256 devices in a mesh: scan: 16 (over x, y_lo, core), cuts: 16 (over y_hi, z).
Axes of the slice: x: 4, y: 4 (y_hi: 2, y_lo: 2; y = y_hi * 2 + y_lo), z: 8, core: 2. Of those that a mesh axis runs over, the one named last changes fastest.
Arguments:
- partials: bfloat16 [16, 2, 96, 128, 2048], P('scan', None, 'cuts'), may hold values from -1.5 to 1.5
- inverses: bfloat16 [8, 96, 96], replicated, may hold values from -0.625 to 0.625
- classes: int32 [128, 2048], P('scan', 'cuts'), may hold values from 0 to 7
Outputs:
- object_update: float32 [2, 96, 128, 2048], P(None, 'cuts', 'scan')
The draws below stay inside these ranges and needn't reach their ends.
All inputs are finite; a program needn't handle non-finite values.
Results may differ from the reference program's by a relative error of at most 0.0031.
Values may be sent and summed in bfloat16 or wider, within the bound.
No kernel may reach another device: no remote copies, remote signals or barrier semaphores. Data moves between devices by JAX's collectives and lax.ppermute only.
A program may use at most 128 MiB of HBM per device.

```python
import jax
import jax.numpy as jnp
from jax import lax

SL = 96
NX = 2048
K = 8
ITERS = 5
GROUPS = 16
ROWS = 128


def touch_ends(result, rng, smallest, top_value):
    index_at = [jax.random.randint(jax.random.fold_in(rng, axis), (), 0, length) for axis, length in enumerate(result.shape)]
    widest = result.shape.index(max(result.shape))
    neighbour = index_at[:widest] + [(index_at[widest] + 1) % result.shape[widest]] + index_at[widest + 1:]
    return result.at[tuple(index_at)].set(smallest).at[tuple(neighbour)].set(top_value)


def raised(array, stream_key, source, target, blocks, factor):
    def block_of(dim):
        return (jnp.arange(array.shape[dim]) // (array.shape[dim] // blocks)).reshape((-1,) + (1,) * (array.ndim - 1 - dim))

    first = jax.random.permutation(stream_key, blocks)[block_of(target)]
    far = (block_of(target) + blocks // 2) % blocks
    return jnp.where((block_of(source) == first) | (block_of(source) == far), factor * array, array)


def level_of(stream_key, shape, shards, smallest, high):
    loudness, own = 1.0, jax.random.fold_in(stream_key, 6)
    for position, blocks in shards:
        draws = jnp.exp(jax.random.uniform(jax.random.fold_in(own, position), (blocks,), jnp.float32, smallest / len(shards), high / len(shards)))
        loudness = loudness * jnp.repeat(draws, shape[position] // blocks).reshape([-1 if axis == position else 1 for axis in range(len(shape))])
    return loudness


def normal_values(key, shape, scale, reach, shards=(), held_as=jnp.bfloat16):
    loudness = level_of(key, shape, shards, -0.22, 0.18) if shards else 1.0
    drawn = jax.random.normal(key, shape, jnp.float32) * scale * loudness
    return jnp.minimum(jnp.maximum(drawn, -reach), reach).astype(held_as)


def noise_with(rng, extent, scale, most, shards, heavy, kind=jnp.bfloat16):
    result = scale * jax.random.normal(rng, extent, jnp.float32)
    if shards:
        result = result * level_of(rng, extent, shards, -0.22, 0.18)
    return jnp.clip(raised(result, jax.random.fold_in(rng, 3), *heavy), -most, most).astype(kind)


def setup_inputs(seed: int = 0) -> dict:
    arg_keys = jax.random.split(jax.random.key(seed), 4)
    partials = noise_with(arg_keys[0], (GROUPS, 2, SL, ROWS, NX), 0.25, 1.5, ((0, 16), (2, 16)), (0, 3, 16, 2.0))
    inverses = normal_values(arg_keys[1], (K, SL, SL), SL ** -0.5, 0.625)
    classes = touch_ends(jax.random.randint(arg_keys[2], (ROWS, NX), 0, K), jax.random.fold_in(arg_keys[2], 1), 0, K - 1).astype(jnp.int32)
    return dict(partials=partials, inverses=inverses, classes=classes)


def tv_step(field, row_first, rows_total):
    count = field.shape[2]
    width = field.shape[3]
    rows = row_first + jnp.arange(count, dtype=jnp.int32)
    cols = jnp.arange(width, dtype=jnp.int32)
    row_ok = ((rows >= 0) & (rows <= rows_total - 2)).astype(jnp.float32)[:, None]
    col_ok = (cols <= width - 2).astype(jnp.float32)
    zero_row = jnp.zeros_like(field[:, :, :1, :])
    zero_col = jnp.zeros_like(field[:, :, :, :1])
    grad_y = (jnp.concatenate([field[:, :, 1:, :], zero_row], axis=2) - field) * row_ok
    grad_x = (jnp.concatenate([field[:, :, :, 1:], zero_col], axis=3) - field) * col_ok
    magnitude = jnp.sqrt(lax.optimization_barrier(jnp.sum(grad_x * grad_x + grad_y * grad_y, axis=0, keepdims=True)) + 1.0)
    flux_y = grad_y / magnitude
    flux_x = grad_x / magnitude
    spread = flux_y - jnp.concatenate([zero_row, flux_y[:, :, :-1, :]], axis=2)
    spread = spread + flux_x - jnp.concatenate([zero_col, flux_x[:, :, :, :-1]], axis=3)
    return field + 0.2 * spread

def reference(partials, inverses, classes):

    def add_group(index, total):
        piece = lax.dynamic_index_in_dim(partials, index, 0, keepdims=False)
        return total + piece.astype(jnp.float32)
    start = jnp.zeros(partials.shape[1:], jnp.float32)
    total = lax.fori_loop(0, partials.shape[0], add_group, start)
    grad = total.astype(jnp.bfloat16).astype(jnp.float32)
    weights = inverses.astype(jnp.float32)
    filtered = jnp.zeros_like(grad)
    for klass in range(K):
        term = jnp.einsum('ij,cjrx->cirx', weights[klass], grad, precision=lax.Precision.HIGHEST, preferred_element_type=jnp.float32)
        filtered = filtered + jnp.where(classes == klass, term, 0.0)
    field = filtered
    for step in range(ITERS):
        field = tv_step(field, 0, field.shape[2])
    return field
```

```python
import jax
import jax.numpy as jnp
from jax import lax
from jax.experimental import pallas as pl
from jax.experimental.pallas import tpu as pltpu
from jax.sharding import PartitionSpec as P

ITERS = 5
SCALE = 32.0


def filter_kernel(grad_ref, weights_ref, classes_ref, out_ref, rows_in, rows_out):
    blocks, parts, depth, rows, lanes = grad_ref.shape
    total = blocks * depth
    kinds = weights_ref.shape[1] // total
    for part in range(parts):
        rows_in[part] = grad_ref[:, part].astype(jnp.float32).reshape(total * rows, lanes)
    weights = weights_ref[...]
    for row in range(rows):
        label = classes_ref[row : row + 1, :]
        label = jnp.concatenate([label] * parts, axis=1)
        values = jnp.concatenate(
            [rows_in[part, pl.ds(row, total, stride=rows), :] for part in range(parts)], axis=1
        )
        masked = jnp.concatenate(
            [jnp.where(label == kind, values, 0.0) for kind in range(kinds)], axis=0
        ).astype(jnp.bfloat16)
        found = jnp.dot(weights, masked, preferred_element_type=jnp.float32)
        for part in range(parts):
            rows_out[part, pl.ds(row, total, stride=rows), :] = found[:, part * lanes : (part + 1) * lanes]
    for part in range(parts):
        out_ref[:, part] = rows_out[part].reshape(blocks, depth, rows, lanes)


def tv_kernel(above_ref, own_ref, below_ref, out_ref, field, result):
    blocks, parts, depth, rows, lanes = own_ref.shape
    halo = ITERS
    step = parts * depth * rows
    first = (lax.axis_index("scan") == 0).astype(jnp.float32)
    last = (lax.axis_index("scan") == lax.axis_size("scan") - 1).astype(jnp.float32)
    lane = lax.broadcasted_iota(jnp.int32, (blocks, lanes), 1)
    block = lax.broadcasted_iota(jnp.int32, (blocks, lanes), 0)
    at_left = lane == 0
    at_right = lane == lanes - 1
    inner = jnp.where(at_right & (block == blocks - 1), 0.0, 1.0)

    def following(cells):
        near = pltpu.roll(cells, lanes - 1, 1)
        return jnp.where(at_right, pltpu.roll(near, blocks - 1, 0), near)

    def preceding(cells):
        near = pltpu.roll(cells, 1, 1)
        return jnp.where(at_left, pltpu.roll(near, 1, 0), near)

    def one_slice(s, carry):
        for row in range(-halo, rows + halo):
            source, at = (above_ref, row + rows) if row < 0 else (own_ref, row) if row < rows else (below_ref, row - rows)
            for part in range(parts):
                field[row + halo, part] = source[:, part, s, at, :]
        for sweep in range(1, ITERS + 1):
            low, high = sweep - ITERS, rows + ITERS - sweep
            before = None
            here = [field[low - 1 + halo, part] for part in range(parts)]
            for row in range(low - 1, high):
                below = [field[row + 1 + halo, part] for part in range(parts)]
                down = [b - h for b, h in zip(below, here)]
                if row == -1:
                    down = [d * (1.0 - first) for d in down]
                if row == rows - 1:
                    down = [d * (1.0 - last) for d in down]
                across = [(following(h) - h) * inner for h in here]
                power = sum(d * d for d in down) + sum(a * a for a in across)
                inverse = lax.rsqrt(power + 1.0)
                flux = [d * inverse for d in down]
                if before is not None:
                    for part in range(parts):
                        side = across[part] * inverse
                        spread = flux[part] - before[part] + side - preceding(side)
                        fresh = here[part] + 0.2 * spread
                        if sweep == ITERS:
                            out_ref[part, s, row, :, :] = fresh
                        else:
                            field[row + halo, part] = fresh
                before = flux
                here = below
        return carry

    lax.fori_loop(0, depth, one_slice, 0)


def on_device(partials, inverses, classes):
    _, parts, depth, rows_total, width = partials.shape
    scans = lax.axis_size("scan")
    cuts = lax.axis_size("cuts")
    rows = rows_total // scans
    lanes = width // cuts
    kinds, total, _ = inverses.shape
    core = lax.axis_index("scan") % 2

    split = partials.reshape(parts, depth, scans // 2, 2, rows, width)
    give = lax.dynamic_index_in_dim(split, 1 - core, 3, keepdims=False)
    keep = lax.dynamic_index_in_dim(split, core, 3, keepdims=False)
    got = lax.ppermute(give, "scan", [(i, i ^ 1) for i in range(scans)])
    pair = (keep.astype(jnp.float32) + got.astype(jnp.float32)).astype(jnp.bfloat16)
    pair = pair.transpose(2, 0, 1, 3, 4)
    groups = [list(range(c, scans, 2)) for c in range(2)]
    terms = lax.all_to_all(pair, "scan", 0, 0, axis_index_groups=groups, tiled=True)
    grad = jnp.sum(terms.astype(jnp.float32), axis=0).astype(jnp.bfloat16)

    grad = grad.reshape(parts, depth, rows, cuts, lanes).transpose(3, 0, 1, 2, 4)
    grad = lax.all_to_all(grad, "cuts", 0, 0, tiled=True)
    weights = inverses.transpose(1, 0, 2).reshape(total, kinds * total)
    filtered = pl.pallas_call(
        filter_kernel,
        out_shape=jax.ShapeDtypeStruct(grad.shape, jnp.float32),
        scratch_shapes=[
            pltpu.VMEM((parts, total * rows, lanes), jnp.float32),
            pltpu.VMEM((parts, total * rows, lanes), jnp.float32),
        ],
        compiler_params=pltpu.CompilerParams(vmem_limit_bytes=32 * 1024 * 1024),
    )(grad, weights, classes)
    coded = (filtered * SCALE).astype(jnp.float16)
    coded = lax.all_to_all(coded, "cuts", 0, 0, tiled=True)
    above = lax.ppermute(coded, "scan", [(i, i + 1) for i in range(scans - 1)])
    below = lax.ppermute(coded, "scan", [(i + 1, i) for i in range(scans - 1)])
    above, own, below = [c.astype(jnp.float32) * (1.0 / SCALE) for c in (above, coded, below)]
    result = pl.pallas_call(
        tv_kernel,
        out_shape=jax.ShapeDtypeStruct((parts, depth, rows, cuts, lanes), jnp.float32),
        scratch_shapes=[
            pltpu.VMEM((rows + 2 * ITERS, parts, cuts, lanes), jnp.float32),
            pltpu.VMEM((8, lanes), jnp.float32),
        ],
        compiler_params=pltpu.CompilerParams(vmem_limit_bytes=32 * 1024 * 1024),
    )(above, own, below)
    return result.reshape(parts, depth, rows, width)


def solution(mesh):
    placed = (P("scan", None, "cuts", None, None), P(), P("scan", "cuts"))
    return jax.shard_map(
        on_device,
        mesh=mesh,
        in_specs=placed,
        out_specs=P(None, "cuts", "scan", None),
        check_vma=False,
    )
```

```python
import jax
import jax.numpy as jnp
from jax import lax
from jax.experimental import pallas as pl
from jax.experimental.pallas import tpu as pltpu
from jax.sharding import PartitionSpec as P

ITERS = 5
TILE = 16
SUM_SCALE = 1024.0
SCALE = 32.0


def filter_kernel(grad_ref, weights_ref, classes_ref, out_ref, cells):
    blocks, parts, depth, rows, lanes = grad_ref.shape
    total = blocks * depth
    kinds = weights_ref.shape[1] // total
    for part in range(parts):
        cells[part] = grad_ref[:, part].astype(jnp.float32).reshape(total * rows, lanes)
    weights = weights_ref[...]
    for row in range(rows):
        label = classes_ref[row : row + 1, :]
        label = jnp.concatenate([label] * parts, axis=1)
        values = jnp.concatenate(
            [cells[part, pl.ds(row, total, stride=rows), :] for part in range(parts)], axis=1
        )
        masked = jnp.concatenate(
            [jnp.where(label == kind, values, 0.0) for kind in range(kinds)], axis=0
        ).astype(jnp.bfloat16)
        found = jnp.dot(weights, masked, preferred_element_type=jnp.float32)
        for part in range(parts):
            for s in range(depth):
                out_ref[pl.ds((row * parts + part) * depth + s, blocks, stride=rows * parts * depth), :] = found[
                    s * blocks : (s + 1) * blocks, part * lanes : (part + 1) * lanes
                ]


def tv_kernel(shape, skipped, above_ref, own_ref, below_ref, out_ref, field):
    blocks, parts, depth, rows, lanes = shape
    halo = ITERS
    half = blocks // 2
    first = (lax.axis_index("scan") == 0).astype(jnp.float32)
    last = (lax.axis_index("scan") == lax.axis_size("scan") - 1).astype(jnp.float32)
    lane = lax.broadcasted_iota(jnp.int32, (half, lanes), 1)
    line = lax.broadcasted_iota(jnp.int32, (half, lanes), 0)
    at_left = lane == 0
    at_right = lane == lanes - 1
    inner = jnp.where(at_right & (line == half - 1), 0.0, 1.0)

    def following(pair):
        near = [pltpu.roll(p, lanes - 1, 1) for p in pair]
        return jnp.where(at_right, near[1], near[0]), jnp.where(at_right, pltpu.roll(near[0], half - 1, 0), near[1])

    def preceding(pair):
        near = [pltpu.roll(p, 1, 1) for p in pair]
        return jnp.where(at_left, pltpu.roll(near[1], 1, 0), near[0]), jnp.where(at_left, near[0], near[1])

    def load(s, row, part, side):
        if row < 0:
            source, at = above_ref, (row + rows) * parts * depth - skipped
        elif row < rows:
            source, at = own_ref, row * parts * depth
        else:
            source, at = below_ref, (row - rows) * parts * depth
        per = source.shape[0] // blocks
        return source[pl.ds(side * per + at + part * depth + s, half, stride=2 * per), :]

    def one_slice(s, carry):
        for sweep in range(1, ITERS + 1):
            low, high = sweep - ITERS, rows + ITERS - sweep

            def read(row):
                if sweep == 1:
                    return [[load(s, row, part, side) for side in range(2)] for part in range(parts)]
                return [[field[row + halo, part, side] for side in range(2)] for part in range(parts)]

            before = None
            here = read(low - 1)
            for row in range(low - 1, high):
                below = read(row + 1)
                flux, across, inverse = [], [], []
                down = [[b - h for b, h in zip(bs, hs)] for bs, hs in zip(below, here)]
                if row == -1:
                    down = [[d * (1.0 - first) for d in ds] for ds in down]
                if row == rows - 1:
                    down = [[d * (1.0 - last) for d in ds] for ds in down]
                for part in range(parts):
                    after = following(here[part])
                    across.append([after[0] - here[part][0], (after[1] - here[part][1]) * inner])
                for side in range(2):
                    power = 1.0
                    for part in range(parts):
                        power = power + down[part][side] * down[part][side] + across[part][side] * across[part][side]
                    inverse.append(lax.rsqrt(power))
                flux = [[d * i for d, i in zip(ds, inverse)] for ds in down]
                if before is not None:
                    for part in range(parts):
                        sides = [a * i for a, i in zip(across[part], inverse)]
                        earlier = preceding(sides)
                        for side in range(2):
                            spread = flux[part][side] - before[part][side] + sides[side] - earlier[side]
                            fresh = here[part][side] + 0.2 * spread
                            if sweep == ITERS:
                                out_ref[part * depth + s, pl.ds(side * rows + row, half, stride=2 * rows), :] = fresh
                            else:
                                field[row + halo, part, side] = fresh
                before = flux
                here = below
        return carry

    lax.fori_loop(0, depth, one_slice, 0)


def on_device(partials, inverses, classes):
    _, parts, depth, rows_total, width = partials.shape
    scans = lax.axis_size("scan")
    cuts = lax.axis_size("cuts")
    rows = rows_total // scans
    lanes = width // cuts
    kinds, total, _ = inverses.shape
    me = lax.axis_index("scan")
    core, y, x = me % 2, (me // 2) % 2, me // 4
    chips = scans // 4
    f32, f16 = jnp.float32, jnp.float16

    def pick(array, index, axis):
        return lax.dynamic_index_in_dim(array, index, axis, keepdims=False)

    def send(array, target):
        return lax.ppermute(array, "scan", [(i, target(i)) for i in range(scans)])

    def other_core(i):
        return i ^ 1

    def other_y(i):
        return i ^ 2

    def along_x(k):
        return lambda i: (i + 4 * k) % scans

    def add(*terms):
        return sum(t.astype(f32) for t in terms)

    split = partials.reshape(parts, depth, chips, 2, 2, rows, width)

    give = pick(split, 1 - core, 4)
    mine = pick(split, core, 4)
    far = send(pick(give[1], 1 - y, 2), other_core)
    all_x = send(give[0], other_core)
    near = send(pick(give[1], y, 2), other_core)

    away = (add(pick(mine[1], 1 - y, 2), far) * SUM_SCALE).astype(f16)
    came = send(away, other_y)

    sums = [
        (add(pick(mine[0], (x + k) % chips, 1), pick(all_x, (x + k) % chips, 1)) * SUM_SCALE).astype(f16)
        for k in range(1, chips)
    ]
    order = sorted(range(1, chips), key=lambda k: abs(k - chips // 2))
    from_x = [send(sums[k - 1], along_x(k)) for k in order]
    kept = add(pick(mine[0], x, 1), pick(all_x, x, 1)) * SUM_SCALE
    over_x = kept + add(*from_x)
    from_y = send(pick(over_x, 1 - y, 1).astype(f16), other_y)
    part0 = pick(over_x, y, 1) + from_y.astype(f32)

    own = add(pick(mine[1], y, 2), near) * SUM_SCALE
    over_y = own + came.astype(f32)
    sent = [send(pick(over_y, (x + k) % chips, 1).astype(f16), along_x(k)) for k in order]
    part1 = pick(over_y, x, 1) + add(*sent)

    grad = (jnp.stack([part0, part1]) * (1.0 / SUM_SCALE)).astype(jnp.bfloat16)
    grad = grad.reshape(parts, depth, rows, cuts, lanes).transpose(3, 0, 1, 2, 4)
    grad = lax.all_to_all(grad, "cuts", 0, 0, tiled=True)
    weights = inverses.reshape(kinds, cuts, depth, total).transpose(2, 1, 0, 3).reshape(total, kinds * total)
    per = rows * parts * depth
    filtered = pl.pallas_call(
        filter_kernel,
        out_shape=jax.ShapeDtypeStruct((cuts * per, lanes), f32),
        scratch_shapes=[pltpu.VMEM((parts, total * rows, lanes), f32)],
        compiler_params=pltpu.CompilerParams(vmem_limit_bytes=32 * 1024 * 1024),
    )(grad, weights, classes)
    coded = (filtered * SCALE).astype(f16).reshape(cuts, per, lanes)
    coded = lax.all_to_all(coded, "cuts", 0, 0, tiled=True)
    skipped = (rows - ITERS) * parts * depth // TILE * TILE
    needed = -(-ITERS * parts * depth // TILE) * TILE
    above = lax.ppermute(coded[:, skipped:], "scan", [(i, i + 1) for i in range(scans - 1)])
    below = lax.ppermute(coded[:, :needed], "scan", [(i + 1, i) for i in range(scans - 1)])
    above, middle, below = [
        (c.astype(f32) * (1.0 / SCALE)).reshape(-1, lanes) for c in (above, coded, below)
    ]
    shape = (cuts, parts, depth, rows, lanes)
    result = pl.pallas_call(
        lambda *refs: tv_kernel(shape, skipped, *refs),
        out_shape=jax.ShapeDtypeStruct((parts * depth, cuts * rows, lanes), f32),
        scratch_shapes=[pltpu.VMEM((rows + 2 * ITERS, parts, 2, cuts // 2, lanes), f32)],
        compiler_params=pltpu.CompilerParams(vmem_limit_bytes=32 * 1024 * 1024),
    )(above, middle, below)
    result = result.reshape(parts, depth, cuts, rows, lanes).transpose(0, 1, 3, 2, 4)
    return result.reshape(parts, depth, rows, width)


def solution(mesh):
    placed = (P("scan", None, "cuts", None, None), P(), P("scan", "cuts"))
    return jax.shard_map(
        on_device,
        mesh=mesh,
        in_specs=placed,
        out_specs=P(None, "cuts", "scan", None),
        check_vma=False,
    )
```

```python
import jax
import jax.numpy as jnp
from jax import lax
from jax.experimental import pallas as pl
from jax.experimental.pallas import tpu as pltpu
from jax.sharding import PartitionSpec as P

ITERS = 5
TILE = 16
SUM_SCALE = 1024.0
SCALE = 32.0


def filter_kernel(grad_ref, weights_ref, classes_ref, out_ref, cells):
    blocks, parts, depth, rows, lanes = grad_ref.shape
    total = blocks * depth
    kinds = weights_ref.shape[1] // total
    for part in range(parts):
        cells[part] = grad_ref[:, part].astype(jnp.float32).reshape(total * rows, lanes)
    weights = weights_ref[...]
    for row in range(rows):
        label = classes_ref[row : row + 1, :]
        label = jnp.concatenate([label] * parts, axis=1)
        values = jnp.concatenate(
            [cells[part, pl.ds(row, total, stride=rows), :] for part in range(parts)], axis=1
        )
        masked = jnp.concatenate(
            [jnp.where(label == kind, values, 0.0) for kind in range(kinds)], axis=0
        ).astype(jnp.bfloat16)
        found = jnp.dot(weights, masked, preferred_element_type=jnp.float32)
        for part in range(parts):
            for s in range(depth):
                out_ref[pl.ds((row * parts + part) * depth + s, blocks, stride=rows * parts * depth), :] = found[
                    s * blocks : (s + 1) * blocks, part * lanes : (part + 1) * lanes
                ]


def tv_kernel(shape, skipped, above_ref, own_ref, below_ref, out_ref, field):
    blocks, parts, depth, rows, lanes = shape
    halo = ITERS
    half = blocks // 2
    first = (lax.axis_index("scan") == 0).astype(jnp.float32)
    last = (lax.axis_index("scan") == lax.axis_size("scan") - 1).astype(jnp.float32)
    lane = lax.broadcasted_iota(jnp.int32, (half, lanes), 1)
    line = lax.broadcasted_iota(jnp.int32, (half, lanes), 0)
    at_left = lane == 0
    at_right = lane == lanes - 1
    inner = jnp.where(at_right & (line == half - 1), 0.0, 1.0)

    def following(pair):
        near = [pltpu.roll(p, lanes - 1, 1) for p in pair]
        return jnp.where(at_right, near[1], near[0]), jnp.where(at_right, pltpu.roll(near[0], half - 1, 0), near[1])

    def preceding(pair):
        near = [pltpu.roll(p, 1, 1) for p in pair]
        return jnp.where(at_left, pltpu.roll(near[1], 1, 0), near[0]), jnp.where(at_left, near[0], near[1])

    def load(s, row, part, side):
        if row < 0:
            source, at = above_ref, (row + rows) * parts * depth - skipped
        elif row < rows:
            source, at = own_ref, row * parts * depth
        else:
            source, at = below_ref, (row - rows) * parts * depth
        per = source.shape[0] // blocks
        return source[pl.ds(side * per + at + part * depth + s, half, stride=2 * per), :]

    def one_slice(s, carry):
        for sweep in range(1, ITERS + 1):
            low, high = sweep - ITERS, rows + ITERS - sweep

            def read(row):
                if sweep == 1:
                    return [[load(s, row, part, side) for side in range(2)] for part in range(parts)]
                return [[field[row + halo, part, side] for side in range(2)] for part in range(parts)]

            before = None
            here = read(low - 1)
            for row in range(low - 1, high):
                below = read(row + 1)
                flux, across, inverse = [], [], []
                down = [[b - h for b, h in zip(bs, hs)] for bs, hs in zip(below, here)]
                if row == -1:
                    down = [[d * (1.0 - first) for d in ds] for ds in down]
                if row == rows - 1:
                    down = [[d * (1.0 - last) for d in ds] for ds in down]
                for part in range(parts):
                    after = following(here[part])
                    across.append([after[0] - here[part][0], (after[1] - here[part][1]) * inner])
                for side in range(2):
                    power = 1.0
                    for part in range(parts):
                        power = power + down[part][side] * down[part][side] + across[part][side] * across[part][side]
                    inverse.append(lax.rsqrt(power))
                flux = [[d * i for d, i in zip(ds, inverse)] for ds in down]
                if before is not None:
                    for part in range(parts):
                        sides = [a * i for a, i in zip(across[part], inverse)]
                        earlier = preceding(sides)
                        for side in range(2):
                            spread = flux[part][side] - before[part][side] + sides[side] - earlier[side]
                            fresh = here[part][side] + 0.2 * spread
                            if sweep == ITERS:
                                out_ref[part * depth + s, pl.ds(side * rows + row, half, stride=2 * rows), :] = fresh
                            else:
                                field[row + halo, part, side] = fresh
                before = flux
                here = below
        return carry

    lax.fori_loop(0, depth, one_slice, 0)


def copy_kernel(plan, source_ref, *refs):
    count = len(plan)
    sems = refs[count]
    me = lax.axis_index("scan")
    core, y, x = lax.rem(me, 2), lax.rem(me // 2, 2), me // 4
    chips = source_ref.shape[2]
    copies = []
    for out, (theirs, pieces) in zip(refs, plan):
        whose = 1 - core if theirs else core
        for slot, (part, k, e) in enumerate(pieces):
            copies.append(
                pltpu.make_async_copy(
                    source_ref.at[part, :, lax.rem(x + k, chips), 1 - y if e else y, whose],
                    out.at[slot],
                    sems.at[len(copies)],
                )
            )
    for copy in copies:
        copy.start()
    for copy in copies:
        copy.wait()


def copied(split, *plan):
    _, depth, _, _, _, rows, width = split.shape
    return pl.pallas_call(
        lambda *refs: copy_kernel(plan, *refs),
        out_shape=[jax.ShapeDtypeStruct((len(pieces), depth, rows, width), split.dtype) for _, pieces in plan],
        in_specs=[pl.BlockSpec(memory_space=pltpu.HBM)],
        out_specs=[pl.BlockSpec(memory_space=pl.ANY if theirs else pltpu.VMEM) for theirs, _ in plan],
        scratch_shapes=[pltpu.SemaphoreType.DMA((sum(len(pieces) for _, pieces in plan),))],
        compiler_params=pltpu.CompilerParams(vmem_limit_bytes=24 * 1024 * 1024),
    )(split)


def on_device(partials, inverses, classes):
    _, parts, depth, rows_total, width = partials.shape
    scans = lax.axis_size("scan")
    cuts = lax.axis_size("cuts")
    rows = rows_total // scans
    lanes = width // cuts
    kinds, total, _ = inverses.shape
    chips = scans // 4
    f32, f16 = jnp.float32, jnp.float16

    def send(array, target, order=1):
        return lax.ppermute(array, "scan", [(i, target(i)) for i in range(scans)][::order])

    def other_core(i):
        return i ^ 1

    def other_y(i):
        return i ^ 2

    def along_x(k):
        return lambda i: (i + 4 * k) % scans

    def paired(own, got):
        return (own.astype(f32) + got.astype(f32)) * SUM_SCALE

    weights = inverses.reshape(kinds, cuts, depth, total).transpose(2, 1, 0, 3).reshape(total, kinds * total)

    split = partials.reshape(parts, depth, chips, 2, 2, rows, width)
    split = pltpu.with_memory_space_constraint(split, pltpu.HBM)
    odd = list(range(1, chips, 2))
    even = list(range(2, chips, 2)) + [0]
    along = [(0, k, e) for k in range(1, chips) for e in range(2)]
    across_odd = [(1, k, 1) for k in odd]
    across_even = [(1, k, 1) for k in even]
    kept_along = [(0, 0, 0), (0, 0, 1)]
    kept_odd = [(1, k, 0) for k in odd]
    kept_even = [(1, k, 0) for k in even]
    rest = across_even + kept_odd + kept_even + kept_along
    give_odd, give_along = copied(split, (True, across_odd), (True, along))
    got_odd = send(give_odd, other_core)
    got_along = send(give_along, other_core, -1)
    own_odd, own_along, own_even, own_kept_odd, own_kept_even, own_kept_along, give_rest = copied(
        split,
        (False, across_odd),
        (False, along),
        (False, across_even),
        (False, kept_odd),
        (False, kept_even),
        (False, kept_along),
        (True, rest),
    )
    got_rest = send(give_rest, other_core)
    got_even, got_kept_odd, got_kept_even, got_kept_along = [
        got_rest[2 * i : 2 * i + 2] for i in range(4)
    ]

    def after(value, made):
        return lax.optimization_barrier((value, made))[0]

    sums = paired(own_along, got_along).astype(f16)
    from_x = [send(sums[2 * k - 2 : 2 * k], along_x(k)) for k in range(1, chips)]
    odd_code = paired(own_odd, got_odd).astype(f16)
    came_odd = send(odd_code, other_y)
    even_code = paired(own_even, got_even).astype(f16)
    came_even = send(even_code, other_y, -1)

    came_odd = after(came_odd, even_code)
    odd_sums = (paired(own_kept_odd, got_kept_odd) + came_odd.astype(f32)).astype(f16)
    sent = [send(odd_sums[i], along_x(k), -1) for i, k in enumerate(odd)]

    from_x = after(from_x, odd_sums)
    over_x = paired(own_kept_along, got_kept_along) + sum(c.astype(f32) for c in from_x)
    last = over_x[1].astype(f16)
    part0 = over_x[0] + send(last, other_y).astype(f32)

    came_even = after(came_even, last)
    even_sums = paired(own_kept_even, got_kept_even) + came_even.astype(f32)
    sent += [send(even_sums[i].astype(f16), along_x(k), -1) for i, k in enumerate(even[:-1])]
    part1 = even_sums[len(even) - 1] + sum(c.astype(f32) for c in sent)

    grad = (jnp.stack([part0, part1]) * (1.0 / SUM_SCALE)).astype(jnp.bfloat16)
    grad = grad.reshape(parts, depth, rows, cuts, lanes).transpose(3, 0, 1, 2, 4)
    grad, weights = lax.optimization_barrier((grad, weights))
    grad = lax.all_to_all(grad, "cuts", 0, 0, tiled=True)
    per = rows * parts * depth
    filtered = pl.pallas_call(
        filter_kernel,
        out_shape=jax.ShapeDtypeStruct((cuts * per, lanes), f32),
        scratch_shapes=[pltpu.VMEM((parts, total * rows, lanes), f32)],
        compiler_params=pltpu.CompilerParams(vmem_limit_bytes=32 * 1024 * 1024),
    )(grad, weights, classes)
    coded = (filtered * SCALE).astype(f16).reshape(cuts, per, lanes)
    coded = lax.all_to_all(coded, "cuts", 0, 0, tiled=True)
    skipped = (rows - ITERS) * parts * depth // TILE * TILE
    needed = -(-ITERS * parts * depth // TILE) * TILE
    above = lax.ppermute(coded[:, skipped:], "scan", [(i, i + 1) for i in range(scans - 1)])
    below = lax.ppermute(coded[:, :needed], "scan", [(i + 1, i) for i in range(scans - 1)])
    above, middle, below = [
        (c.astype(f32) * (1.0 / SCALE)).reshape(-1, lanes) for c in (above, coded, below)
    ]
    shape = (cuts, parts, depth, rows, lanes)
    result = pl.pallas_call(
        lambda *refs: tv_kernel(shape, skipped, *refs),
        out_shape=jax.ShapeDtypeStruct((parts * depth, cuts * rows, lanes), f32),
        scratch_shapes=[pltpu.VMEM((rows + 2 * ITERS, parts, 2, cuts // 2, lanes), f32)],
        compiler_params=pltpu.CompilerParams(vmem_limit_bytes=32 * 1024 * 1024),
    )(above, middle, below)
    result = result.reshape(parts, depth, cuts, rows, lanes).transpose(0, 1, 3, 2, 4)
    return result.reshape(parts, depth, rows, width)


def solution(mesh):
    placed = (P("scan", None, "cuts", None, None), P(), P("scan", "cuts"))
    return jax.shard_map(
        on_device,
        mesh=mesh,
        in_specs=placed,
        out_specs=P(None, "cuts", "scan", None),
        check_vma=False,
    )
```

```python
import jax
import jax.numpy as jnp
from jax import lax
from jax.experimental import pallas as pl
from jax.experimental.pallas import tpu as pltpu
from jax.sharding import PartitionSpec as P

ITERS = 5
WAYS = 4
TILE = 16
SUM_SCALE = 1024.0
SCALE = 32.0


def home(lane, shift, lanes):
    return lanes // WAYS * lax.rem(lax.rem(lane, WAYS) + shift, WAYS) + lane // WAYS


def filter_kernel(grad_ref, weights_ref, classes_ref, out_ref, cells):
    blocks, parts, depth, rows, lanes = grad_ref.shape
    total = blocks * depth
    kinds = weights_ref.shape[1] // total
    shift = lax.rem(lax.axis_index("cuts"), WAYS)
    source = lax.broadcasted_iota(jnp.int32, (lanes, lanes), 0)
    target = lax.broadcasted_iota(jnp.int32, (lanes, lanes), 1)
    turn = jnp.where(home(source, shift, lanes) == target, 1.0, 0.0).astype(jnp.bfloat16)
    for part in range(parts):
        flat = grad_ref[:, part].astype(jnp.float32).reshape(total * rows, lanes).astype(jnp.bfloat16)
        cells[part] = jnp.dot(flat, turn, preferred_element_type=jnp.float32)
    labels = jnp.dot(
        classes_ref[...].astype(jnp.float32).astype(jnp.bfloat16), turn, preferred_element_type=jnp.float32
    )
    weights = weights_ref[...]
    for row in range(rows):
        label = jnp.concatenate([labels[row : row + 1, :]] * parts, axis=1)
        values = jnp.concatenate(
            [cells[part, pl.ds(row, total, stride=rows), :] for part in range(parts)], axis=1
        )
        masked = jnp.concatenate(
            [jnp.where(label == float(kind), values, 0.0) for kind in range(kinds)], axis=0
        ).astype(jnp.bfloat16)
        found = jnp.dot(weights, masked, preferred_element_type=jnp.float32)
        for part in range(parts):
            for s in range(depth):
                out_ref[pl.ds((part * rows + row) * depth + s, blocks, stride=rows * parts * depth), :] = found[
                    s * blocks : (s + 1) * blocks, part * lanes : (part + 1) * lanes
                ]


def tv_kernel(shape, skipped, above_ref, own_ref, below_ref, out_ref, field):
    blocks, parts, depth, rows, lanes = shape
    halo = ITERS
    tiles = range(WAYS)
    groups = blocks // WAYS
    lines = parts * groups
    size = lanes // WAYS
    first = (lax.axis_index("scan") == 0).astype(jnp.float32)
    last = (lax.axis_index("scan") == lax.axis_size("scan") - 1).astype(jnp.float32)
    lane = lax.broadcasted_iota(jnp.int32, (lines, lanes), 1)
    line = lax.broadcasted_iota(jnp.int32, (lines, lanes), 0)
    at_left = lane == 0
    at_right = lane == lanes - 1
    inner = jnp.where(at_right & (lax.rem(line, groups) == groups - 1), 0.0, 1.0)
    homes = [home(lane, b, lanes) for b in tiles]

    def skewed(values):
        found = []
        for m in tiles:
            pick = values[-m % WAYS]
            for group in range(1, WAYS):
                pick = jnp.where(lane // size == group, values[(group - m) % WAYS], pick)
            found.append(pick)
        return found

    def load(s, row):
        if row < 0:
            source, at = above_ref, (row + rows) * depth - skipped
        elif row < rows:
            source, at = own_ref, row * depth
        else:
            source, at = below_ref, (row - rows) * depth
        per = source.shape[0] // (blocks * parts)
        found = skewed([source[pl.ds(b * per + at + s, lines, stride=WAYS * per), :] for b in tiles])
        return [pltpu.roll(f, (lanes - size * m) % lanes, 1) for m, f in enumerate(found)]

    def store(s, row, values):
        values = skewed([pltpu.roll(v, size * m, 1) for m, v in enumerate(values)])
        for b in tiles:
            value = jnp.take_along_axis(values[b], homes[b], axis=1)
            for part in range(parts):
                out_ref[part * depth + s, pl.ds(b * rows + row, groups, stride=WAYS * rows), :] = value[
                    part * groups : (part + 1) * groups
                ]

    def one_slice(s, carry):
        for sweep in range(1, ITERS + 1):
            low, high = sweep - ITERS, rows + ITERS - sweep

            def read(row):
                return load(s, row) if sweep == 1 else [field[row + halo, m] for m in tiles]

            before = None
            here = read(low - 1)
            for row in range(low - 1, high):
                below = read(row + 1)
                down = [b - h for b, h in zip(below, here)]
                if row == -1:
                    down = [d * (1.0 - first) for d in down]
                if row == rows - 1:
                    down = [d * (1.0 - last) for d in down]
                near = pltpu.roll(here[0], lanes - 1, 1)
                near = jnp.where(at_right, pltpu.roll(near, lines - 1, 0), near)
                across = [n - h for n, h in zip(here[1:] + [near], here)]
                across[-1] = across[-1] * inner
                power = [d * d + a * a for d, a in zip(down, across)]
                inverse = [lax.rsqrt(p + pltpu.roll(p, groups, 0) + 1.0) for p in power]
                flux = [d * i for d, i in zip(down, inverse)]
                if before is not None:
                    sides = [a * i for a, i in zip(across, inverse)]
                    near = pltpu.roll(sides[-1], 1, 1)
                    near = jnp.where(at_left, pltpu.roll(near, 1, 0), near)
                    fresh = [
                        h + 0.2 * (f - b + s1 - s0)
                        for h, f, b, s1, s0 in zip(here, flux, before, sides, [near] + sides[:-1])
                    ]
                    if sweep == ITERS:
                        store(s, row, fresh)
                    else:
                        for m in tiles:
                            field[row + halo, m] = fresh[m]
                before = flux
                here = below
        return carry

    lax.fori_loop(0, depth, one_slice, 0)


def copy_kernel(plan, source_ref, *refs):
    count = len(plan)
    sems = refs[count]
    me = lax.axis_index("scan")
    core, y, x = lax.rem(me, 2), lax.rem(me // 2, 2), me // 4
    chips = source_ref.shape[2]
    copies = []
    for out, (theirs, pieces) in zip(refs, plan):
        whose = 1 - core if theirs else core
        for slot, (part, k, e) in enumerate(pieces):
            copies.append(
                pltpu.make_async_copy(
                    source_ref.at[part, :, lax.rem(x + k, chips), 1 - y if e else y, whose],
                    out.at[slot],
                    sems.at[len(copies)],
                )
            )
    for copy in copies:
        copy.start()
    for copy in copies:
        copy.wait()


def copied(split, *plan):
    _, depth, _, _, _, rows, width = split.shape
    moved = 4 * sum(len(pieces) for _, pieces in plan) * depth * rows * width
    return pl.pallas_call(
        lambda *refs: copy_kernel(plan, *refs),
        out_shape=[jax.ShapeDtypeStruct((len(pieces), depth, rows, width), split.dtype) for _, pieces in plan],
        in_specs=[pl.BlockSpec(memory_space=pltpu.HBM)],
        out_specs=[pl.BlockSpec(memory_space=pltpu.VMEM)] * len(plan),
        scratch_shapes=[pltpu.SemaphoreType.DMA((sum(len(pieces) for _, pieces in plan),))],
        cost_estimate=pl.CostEstimate(flops=0, bytes_accessed=moved, transcendentals=0),
        compiler_params=pltpu.CompilerParams(vmem_limit_bytes=24 * 1024 * 1024),
    )(split)


def on_device(partials, inverses, classes):
    _, parts, depth, rows_total, width = partials.shape
    scans = lax.axis_size("scan")
    cuts = lax.axis_size("cuts")
    rows = rows_total // scans
    lanes = width // cuts
    kinds, total, _ = inverses.shape
    chips = scans // 4
    f32, f16 = jnp.float32, jnp.float16

    def send(array, target, order=1):
        return lax.ppermute(array, "scan", [(i, target(i)) for i in range(scans)][::order])

    def other_core(i):
        return i ^ 1

    def other_y(i):
        return i ^ 2

    def along_x(k):
        return lambda i: (i + 4 * k) % scans

    def paired(own, got):
        return (own.astype(f32) + got.astype(f32)) * SUM_SCALE

    weights = inverses.reshape(kinds, cuts, depth, total).transpose(2, 1, 0, 3).reshape(total, kinds * total)

    def after(value, made):
        return lax.optimization_barrier((value, made))[0]

    split = partials.reshape(parts, depth, chips, 2, 2, rows, width)
    split = pltpu.with_memory_space_constraint(split, pltpu.HBM)
    early = [(0, 2, 0), (0, 2, 1), (1, 2, 1), (1, 0, 1)]
    late = [(1, 1, 1), (1, 3, 1)] + [(0, k, e) for k in (1, 3, 0) for e in range(2)] + [(1, k, 0) for k in (2, 0, 1, 3)]
    give_early, own_early = copied(split, (True, early), (False, early))
    got_early = send(give_early, other_core)
    give_late, own_late = copied(split, (True, late), (False, late))
    got_late = send(after(give_late, got_early), other_core, -1)

    two_steps = paired(own_early[:2], got_early[:2]).astype(f16)
    y_far = paired(own_early[2:], got_early[2:]).astype(f16)
    came_far = send(y_far, other_y)
    from_left = send(two_steps[0], along_x(1))
    from_right = send(two_steps[1], along_x(3))

    y_near = paired(own_late[:2], got_late[:2]).astype(f16)
    came_near = send(y_near, other_y, -1)
    one_step = paired(own_late[2:6], got_late[2:6])
    mine0 = paired(own_late[6:8], got_late[6:8])
    mine1 = paired(own_late[8:], got_late[8:])

    from_left, from_right = after((from_left, from_right), y_near)
    to_right = jnp.stack([one_step[0] + from_left.astype(f32), one_step[1]]).astype(f16)
    to_left = jnp.stack([one_step[2], one_step[3] + from_right.astype(f32)]).astype(f16)
    x_left = send(to_right, along_x(1))
    x_right = send(to_left, along_x(3))

    came_far = after(came_far, (to_right, to_left))
    far1 = mine1[:2] + came_far.astype(f32)
    two_steps1 = far1[0].astype(f16)
    half = depth // 2
    from_left1 = send(two_steps1[:half], along_x(1), -1)
    from_right1 = send(two_steps1[half:], along_x(3), -1)

    x_left, x_right = after((x_left, x_right), two_steps1)
    over_x = mine0 + x_left.astype(f32) + x_right.astype(f32)
    last = over_x[1].astype(f16)
    part0 = over_x[0] + send(last, other_y).astype(f32)

    came_near, from_left1, from_right1 = after((came_near, from_left1, from_right1), last)
    near1 = mine1[2:] + came_near.astype(f32)
    to_right1 = jnp.concatenate([near1[0, :half] + from_left1.astype(f32), near1[0, half:]]).astype(f16)
    to_left1 = jnp.concatenate([near1[1, :half], near1[1, half:] + from_right1.astype(f32)]).astype(f16)
    x_left1 = send(to_right1, along_x(1))
    x_right1 = send(to_left1, along_x(3))
    part1 = far1[1] + x_left1.astype(f32) + x_right1.astype(f32)

    grad = (jnp.stack([part0, part1]) * (1.0 / SUM_SCALE)).astype(jnp.bfloat16)
    grad = grad.reshape(parts, depth, rows, cuts, lanes).transpose(3, 0, 1, 2, 4)
    grad, weights = lax.optimization_barrier((grad, weights))
    grad = lax.all_to_all(grad, "cuts", 0, 0, tiled=True)
    per = rows * parts * depth
    filtered = pl.pallas_call(
        filter_kernel,
        out_shape=jax.ShapeDtypeStruct((cuts * per, lanes), f32),
        scratch_shapes=[pltpu.VMEM((parts, total * rows, lanes), f32)],
        compiler_params=pltpu.CompilerParams(vmem_limit_bytes=32 * 1024 * 1024),
    )(grad, weights, classes)
    coded = (filtered * SCALE).astype(f16).reshape(cuts, per, lanes)
    coded = lax.all_to_all(coded, "cuts", 0, 0, tiled=True)
    coded = coded.reshape(cuts, parts, rows * depth, lanes)
    skipped = (rows - ITERS) * depth // TILE * TILE
    needed = -(-ITERS * depth // TILE) * TILE
    above = lax.ppermute(coded[:, :, skipped:], "scan", [(i, i + 1) for i in range(scans - 1)])
    below = lax.ppermute(coded[:, :, :needed], "scan", [(i + 1, i) for i in range(scans - 1)])
    above, middle, below = [
        (c.astype(f32) * (1.0 / SCALE)).transpose(1, 0, 2, 3).reshape(-1, lanes) for c in (above, coded, below)
    ]
    shape = (cuts, parts, depth, rows, lanes)
    result = pl.pallas_call(
        lambda *refs: tv_kernel(shape, skipped, *refs),
        out_shape=jax.ShapeDtypeStruct((parts * depth, cuts * rows, lanes), f32),
        scratch_shapes=[pltpu.VMEM((rows + 2 * ITERS, WAYS, parts * cuts // WAYS, lanes), f32)],
        compiler_params=pltpu.CompilerParams(vmem_limit_bytes=32 * 1024 * 1024),
    )(above, middle, below)
    result = result.reshape(parts, depth, cuts, rows, lanes).transpose(0, 1, 3, 2, 4)
    return result.reshape(parts, depth, rows, width)


def solution(mesh):
    placed = (P("scan", None, "cuts", None, None), P(), P("scan", "cuts"))
    return jax.shard_map(
        on_device,
        mesh=mesh,
        in_specs=placed,
        out_specs=P(None, "cuts", "scan", None),
        check_vma=False,
    )
```

```python
import jax
import jax.numpy as jnp
from jax import lax
from jax.experimental import pallas as pl
from jax.experimental.pallas import tpu as pltpu
from jax.sharding import PartitionSpec as P

ITERS = 5
WAYS = 4
TILE = 16
SUM_SCALE = 1024.0
SCALE = 32.0


def home(lane, shift, lanes):
    return lanes // WAYS * lax.rem(lax.rem(lane, WAYS) + shift, WAYS) + lane // WAYS


def filter_kernel(grad_ref, weights_ref, classes_ref, out_ref, cells):
    blocks, parts, depth, rows, lanes = grad_ref.shape
    total = blocks * depth
    kinds = weights_ref.shape[1] // total
    shift = lax.rem(lax.axis_index("cuts"), WAYS)
    source = lax.broadcasted_iota(jnp.int32, (lanes, lanes), 0)
    target = lax.broadcasted_iota(jnp.int32, (lanes, lanes), 1)
    turn = jnp.where(home(source, shift, lanes) == target, 1.0, 0.0).astype(jnp.bfloat16)
    for part in range(parts):
        flat = grad_ref[:, part].astype(jnp.float32).reshape(total * rows, lanes).astype(jnp.bfloat16)
        cells[part] = jnp.dot(flat, turn, preferred_element_type=jnp.float32)
    labels = jnp.dot(
        classes_ref[...].astype(jnp.float32).astype(jnp.bfloat16), turn, preferred_element_type=jnp.float32
    )
    weights = weights_ref[...]
    for row in range(rows):
        label = jnp.concatenate([labels[row : row + 1, :]] * parts, axis=1)
        values = jnp.concatenate(
            [cells[part, pl.ds(row, total, stride=rows), :] for part in range(parts)], axis=1
        )
        masked = jnp.concatenate(
            [jnp.where(label == float(kind), values, 0.0) for kind in range(kinds)], axis=0
        ).astype(jnp.bfloat16)
        found = jnp.dot(weights, masked, preferred_element_type=jnp.float32)
        for part in range(parts):
            for s in range(depth):
                out_ref[pl.ds((part * rows + row) * depth + s, blocks, stride=rows * parts * depth), :] = found[
                    s * blocks : (s + 1) * blocks, part * lanes : (part + 1) * lanes
                ]


def tv_kernel(shape, skipped, above_ref, own_ref, below_ref, out_ref, field):
    blocks, parts, depth, rows, lanes = shape
    halo = ITERS
    tiles = range(WAYS)
    groups = blocks // WAYS
    lines = parts * groups
    size = lanes // WAYS
    first = (lax.axis_index("scan") == 0).astype(jnp.float32)
    last = (lax.axis_index("scan") == lax.axis_size("scan") - 1).astype(jnp.float32)
    lane = lax.broadcasted_iota(jnp.int32, (lines, lanes), 1)
    line = lax.broadcasted_iota(jnp.int32, (lines, lanes), 0)
    at_left = lane == 0
    at_right = lane == lanes - 1
    inner = jnp.where(at_right & (lax.rem(line, groups) == groups - 1), 0.0, 1.0)
    homes = [home(lane, b, lanes) for b in tiles]

    def skewed(values):
        found = []
        for m in tiles:
            pick = values[-m % WAYS]
            for group in range(1, WAYS):
                pick = jnp.where(lane // size == group, values[(group - m) % WAYS], pick)
            found.append(pick)
        return found

    def load(s, row):
        if row < 0:
            source, at = above_ref, (row + rows) * depth - skipped
        elif row < rows:
            source, at = own_ref, row * depth
        else:
            source, at = below_ref, (row - rows) * depth
        per = source.shape[0] // (blocks * parts)
        found = skewed([source[pl.ds(b * per + at + s, lines, stride=WAYS * per), :] for b in tiles])
        return [pltpu.roll(f, (lanes - size * m) % lanes, 1) for m, f in enumerate(found)]

    def store(s, row, values):
        values = skewed([pltpu.roll(v, size * m, 1) for m, v in enumerate(values)])
        for b in tiles:
            value = jnp.take_along_axis(values[b], homes[b], axis=1)
            for part in range(parts):
                out_ref[part * depth + s, pl.ds(b * rows + row, groups, stride=WAYS * rows), :] = value[
                    part * groups : (part + 1) * groups
                ]

    def one_slice(s, carry):
        for sweep in range(1, ITERS + 1):
            low, high = sweep - ITERS, rows + ITERS - sweep

            def read(row):
                return load(s, row) if sweep == 1 else [field[row + halo, m] for m in tiles]

            before = None
            here = read(low - 1)
            for row in range(low - 1, high):
                below = read(row + 1)
                down = [b - h for b, h in zip(below, here)]
                if row == -1:
                    down = [d * (1.0 - first) for d in down]
                if row == rows - 1:
                    down = [d * (1.0 - last) for d in down]
                near = pltpu.roll(here[0], lanes - 1, 1)
                near = jnp.where(at_right, pltpu.roll(near, lines - 1, 0), near)
                across = [n - h for n, h in zip(here[1:] + [near], here)]
                across[-1] = across[-1] * inner
                power = [d * d + a * a for d, a in zip(down, across)]
                inverse = [lax.rsqrt(p + pltpu.roll(p, groups, 0) + 1.0) for p in power]
                flux = [d * i for d, i in zip(down, inverse)]
                if before is not None:
                    sides = [a * i for a, i in zip(across, inverse)]
                    near = pltpu.roll(sides[-1], 1, 1)
                    near = jnp.where(at_left, pltpu.roll(near, 1, 0), near)
                    fresh = [
                        h + 0.2 * (f - b + s1 - s0)
                        for h, f, b, s1, s0 in zip(here, flux, before, sides, [near] + sides[:-1])
                    ]
                    if sweep == ITERS:
                        store(s, row, fresh)
                    else:
                        for m in tiles:
                            field[row + halo, m] = fresh[m]
                before = flux
                here = below
        return carry

    lax.fori_loop(0, depth, one_slice, 0)


def copy_kernel(plan, source_ref, *refs):
    count = len(plan)
    sems = refs[count]
    me = lax.axis_index("scan")
    core, y, x = lax.rem(me, 2), lax.rem(me // 2, 2), me // 4
    chips = source_ref.shape[2]
    copies = []
    for out, (theirs, pieces) in zip(refs, plan):
        whose = 1 - core if theirs else core
        for slot, (part, k, e) in enumerate(pieces):
            copies.append(
                pltpu.make_async_copy(
                    source_ref.at[part, :, lax.rem(x + k, chips), 1 - y if e else y, whose],
                    out.at[slot],
                    sems.at[len(copies)],
                )
            )
    for copy in copies:
        copy.start()
    for copy in copies:
        copy.wait()


def copied(split, *plan):
    _, depth, _, _, _, rows, width = split.shape
    moved = 4 * sum(len(pieces) for _, pieces in plan) * depth * rows * width
    return pl.pallas_call(
        lambda *refs: copy_kernel(plan, *refs),
        out_shape=[jax.ShapeDtypeStruct((len(pieces), depth, rows, width), split.dtype) for _, pieces in plan],
        in_specs=[pl.BlockSpec(memory_space=pltpu.HBM)],
        out_specs=[pl.BlockSpec(memory_space=pltpu.VMEM)] * len(plan),
        scratch_shapes=[pltpu.SemaphoreType.DMA((sum(len(pieces) for _, pieces in plan),))],
        cost_estimate=pl.CostEstimate(flops=0, bytes_accessed=moved, transcendentals=0),
        compiler_params=pltpu.CompilerParams(vmem_limit_bytes=24 * 1024 * 1024),
    )(split)


def on_device(partials, inverses, classes):
    _, parts, depth, rows_total, width = partials.shape
    scans = lax.axis_size("scan")
    cuts = lax.axis_size("cuts")
    rows = rows_total // scans
    lanes = width // cuts
    kinds, total, _ = inverses.shape
    chips = scans // 4
    f32, f16 = jnp.float32, jnp.float16

    def send(array, target, turn=0):
        pairs = [(i, target(i)) for i in range(scans)]
        return lax.ppermute(array, "scan", pairs[turn:] + pairs[:turn])

    def other_core(i):
        return i ^ 1

    def other_y(i):
        return i ^ 2

    def along_x(k):
        return lambda i: (i + 4 * k) % scans

    def paired(own, got):
        return (own.astype(f32) + got.astype(f32)) * SUM_SCALE

    weights = inverses.reshape(kinds, cuts, depth, total).transpose(2, 1, 0, 3).reshape(total, kinds * total)

    def after(value, made):
        return lax.optimization_barrier((value, made))[0]

    split = partials.reshape(parts, depth, chips, 2, 2, rows, width)
    split = pltpu.with_memory_space_constraint(split, pltpu.HBM)
    early = [(0, 2, 0), (0, 2, 1), (1, 2, 1), (1, 0, 1)]
    late = [(1, 1, 1), (1, 3, 1)] + [(0, k, e) for k in (1, 3, 0) for e in range(2)] + [(1, k, 0) for k in (2, 0, 1, 3)]
    give_early, own_early = copied(split, (True, early), (False, early))
    got_early = send(give_early, other_core)
    give_late, own_late = copied(split, (True, late), (False, late))
    got_late = send(after(give_late, got_early), other_core, 1)

    two_steps = paired(own_early[:2], got_early[:2]).astype(f16)
    y_far = paired(own_early[2:], got_early[2:]).astype(f16)
    came_far = send(y_far, other_y)
    from_left = send(two_steps[0], along_x(1))
    from_right = send(two_steps[1], along_x(3))

    y_near = paired(own_late[:2], got_late[:2]).astype(f16)
    came_near = send(y_near, other_y, 1)
    one_step = paired(own_late[2:6], got_late[2:6])
    mine0 = paired(own_late[6:8], got_late[6:8])
    mine1 = paired(own_late[8:], got_late[8:])

    from_left, from_right = after((from_left, from_right), y_near)
    to_right = jnp.stack([one_step[0] + from_left.astype(f32), one_step[1]]).astype(f16)
    to_left = jnp.stack([one_step[2], one_step[3] + from_right.astype(f32)]).astype(f16)
    x_left = send(to_right, along_x(1))
    x_right = send(to_left, along_x(3))

    came_far = after(came_far, (to_right, to_left))
    far1 = mine1[:2] + came_far.astype(f32)
    two_steps1 = far1[0].astype(f16)
    half = depth // 2
    from_left1 = send(two_steps1[:half], along_x(1), 1)
    from_right1 = send(two_steps1[half:], along_x(3), 1)

    x_left, x_right = after((x_left, x_right), two_steps1)
    over_x = mine0 + x_left.astype(f32) + x_right.astype(f32)
    last = over_x[1].astype(f16)
    part0 = over_x[0] + send(last, other_y, 2).astype(f32)

    came_near, from_left1, from_right1 = after((came_near, from_left1, from_right1), last)
    near1 = mine1[2:] + came_near.astype(f32)
    to_right1 = jnp.concatenate([near1[0, :half] + from_left1.astype(f32), near1[0, half:]]).astype(f16)
    to_left1 = jnp.concatenate([near1[1, :half], near1[1, half:] + from_right1.astype(f32)]).astype(f16)
    x_left1 = send(to_right1, along_x(1), 2)
    x_right1 = send(to_left1, along_x(3), 2)
    x_left1, x_right1 = after((x_left1, x_right1), part0)
    part1 = far1[1] + x_left1.astype(f32) + x_right1.astype(f32)

    grad = (jnp.stack([part0, part1]) * (1.0 / SUM_SCALE)).astype(jnp.bfloat16)
    grad = grad.reshape(parts, depth, rows, cuts, lanes).transpose(3, 0, 1, 2, 4)
    upper = lax.axis_index("scan") & 1 == 0
    grad, weights, upper = lax.optimization_barrier((grad, weights, upper))
    grad = lax.all_to_all(grad, "cuts", 0, 0, tiled=True)
    per = rows * parts * depth
    filtered = pl.pallas_call(
        filter_kernel,
        out_shape=jax.ShapeDtypeStruct((cuts * per, lanes), f32),
        scratch_shapes=[pltpu.VMEM((parts, total * rows, lanes), f32)],
        compiler_params=pltpu.CompilerParams(vmem_limit_bytes=32 * 1024 * 1024),
    )(grad, weights, classes)
    coded = (filtered * SCALE).astype(f16).reshape(cuts, per, lanes)
    coded = lax.all_to_all(coded, "cuts", 0, 0, tiled=True)
    coded = coded.reshape(cuts, parts, rows * depth, lanes)
    skipped = (rows - ITERS) * depth // TILE * TILE
    needed = -(-ITERS * depth // TILE) * TILE
    top, bottom = coded[:, :, :needed], coded[:, :, skipped:]
    odds = range(1, scans - 1, 2)
    chip = lax.ppermute(
        jnp.where(upper, top, bottom), "scan", [(i, i + 1) for i in odds] + [(i + 1, i) for i in odds]
    )
    core = send(jnp.where(upper, bottom, top), other_core)
    above, below = jnp.where(upper, chip, core), jnp.where(upper, core, chip)
    above, middle, below = [
        (c.astype(f32) * (1.0 / SCALE)).transpose(1, 0, 2, 3).reshape(-1, lanes) for c in (above, coded, below)
    ]
    shape = (cuts, parts, depth, rows, lanes)
    result = pl.pallas_call(
        lambda *refs: tv_kernel(shape, skipped, *refs),
        out_shape=jax.ShapeDtypeStruct((parts * depth, cuts * rows, lanes), f32),
        scratch_shapes=[pltpu.VMEM((rows + 2 * ITERS, WAYS, parts * cuts // WAYS, lanes), f32)],
        compiler_params=pltpu.CompilerParams(vmem_limit_bytes=32 * 1024 * 1024),
    )(above, middle, below)
    result = result.reshape(parts, depth, cuts, rows, lanes).transpose(0, 1, 3, 2, 4)
    return result.reshape(parts, depth, rows, width)


def solution(mesh):
    placed = (P("scan", None, "cuts", None, None), P(), P("scan", "cuts"))
    return jax.shard_map(
        on_device,
        mesh=mesh,
        in_specs=placed,
        out_specs=P(None, "cuts", "scan", None),
        check_vma=False,
    )
```

```python
import jax
import jax.numpy as jnp
from jax import lax
from jax.experimental import pallas as pl
from jax.experimental.pallas import tpu as pltpu
from jax.sharding import PartitionSpec as P

ITERS = 5
WAYS = 4
TILE = 16
SUM_SCALE = 1024.0
SCALE = 32.0


def home(lane, shift, lanes):
    return lanes // WAYS * lax.rem(lax.rem(lane, WAYS) + shift, WAYS) + lane // WAYS


def filter_kernel(grad_ref, weights_ref, classes_ref, out_ref, cells):
    blocks, parts, depth, rows, lanes = grad_ref.shape
    total = blocks * depth
    kinds = weights_ref.shape[1] // total
    shift = lax.rem(lax.axis_index("cuts"), WAYS)
    source = lax.broadcasted_iota(jnp.int32, (lanes, lanes), 0)
    target = lax.broadcasted_iota(jnp.int32, (lanes, lanes), 1)
    turn = jnp.where(home(source, shift, lanes) == target, 1.0, 0.0).astype(jnp.bfloat16)
    for part in range(parts):
        flat = grad_ref[:, part].astype(jnp.float32).reshape(total * rows, lanes).astype(jnp.bfloat16)
        cells[part] = jnp.dot(flat, turn, preferred_element_type=jnp.float32)
    labels = jnp.dot(
        classes_ref[...].astype(jnp.float32).astype(jnp.bfloat16), turn, preferred_element_type=jnp.float32
    )
    weights = weights_ref[...]
    for row in range(rows):
        label = jnp.concatenate([labels[row : row + 1, :]] * parts, axis=1)
        values = jnp.concatenate(
            [cells[part, pl.ds(row, total, stride=rows), :] for part in range(parts)], axis=1
        )
        masked = jnp.concatenate(
            [jnp.where(label == float(kind), values, 0.0) for kind in range(kinds)], axis=0
        ).astype(jnp.bfloat16)
        found = jnp.dot(weights, masked, preferred_element_type=jnp.float32)
        for part in range(parts):
            for s in range(depth):
                out_ref[pl.ds((part * rows + row) * depth + s, blocks, stride=rows * parts * depth), :] = found[
                    s * blocks : (s + 1) * blocks, part * lanes : (part + 1) * lanes
                ]


class Tiles:
    def __init__(self, shape):
        self.blocks, self.parts, self.depth, self.rows, self.lanes = shape
        self.groups = self.blocks // WAYS
        self.lines = self.parts * self.groups
        self.size = self.lanes // WAYS
        self.lane = lax.broadcasted_iota(jnp.int32, (self.lines, self.lanes), 1)
        line = lax.broadcasted_iota(jnp.int32, (self.lines, self.lanes), 0)
        self.at_left = self.lane == 0
        self.at_right = self.lane == self.lanes - 1
        self.inner = jnp.where(self.at_right & (lax.rem(line, self.groups) == self.groups - 1), 0.0, 1.0)

    def skewed(self, values):
        found = []
        for m in range(WAYS):
            pick = values[-m % WAYS]
            for group in range(1, WAYS):
                pick = jnp.where(self.lane // self.size == group, values[(group - m) % WAYS], pick)
            found.append(pick)
        return found

    def load(self, source, at):
        per = source.shape[0] // (self.blocks * self.parts)
        found = [source[pl.ds(b * per + at, self.lines, stride=WAYS * per), :] for b in range(WAYS)]
        return [
            pltpu.roll(f, (self.lanes - self.size * m) % self.lanes, 1) for m, f in enumerate(self.skewed(found))
        ]

    def store(self, out_ref, s, row, values):
        values = self.skewed([pltpu.roll(v, self.size * m, 1) for m, v in enumerate(values)])
        for b in range(WAYS):
            value = jnp.take_along_axis(values[b], home(self.lane, b, self.lanes), axis=1)
            for part in range(self.parts):
                out_ref[part * self.depth + s, pl.ds(b * self.rows + row, self.groups, stride=WAYS * self.rows), :] = (
                    value[part * self.groups : (part + 1) * self.groups]
                )

    def sweep(self, low, high, read, write, edges=()):
        before = None
        here = read(low - 1)
        for row in range(low - 1, high):
            below = read(row + 1)
            down = [b - h for b, h in zip(below, here)]
            for edge, factor in edges:
                if row == edge:
                    down = [d * factor for d in down]
            near = pltpu.roll(here[0], self.lanes - 1, 1)
            near = jnp.where(self.at_right, pltpu.roll(near, self.lines - 1, 0), near)
            across = [n - h for n, h in zip(here[1:] + [near], here)]
            across[-1] = across[-1] * self.inner
            power = [d * d + a * a for d, a in zip(down, across)]
            inverse = [lax.rsqrt(p + pltpu.roll(p, self.groups, 0) + 1.0) for p in power]
            flux = [d * i for d, i in zip(down, inverse)]
            if before is not None:
                sides = [a * i for a, i in zip(across, inverse)]
                near = pltpu.roll(sides[-1], 1, 1)
                near = jnp.where(self.at_left, pltpu.roll(near, 1, 0), near)
                fresh = [
                    h + 0.2 * (f - b + s1 - s0)
                    for h, f, b, s1, s0 in zip(here, flux, before, sides, [near] + sides[:-1])
                ]
                write(row, here, fresh)
            before = flux
            here = below


def near_kernel(shape, skipped, own_ref, core_ref, out_ref, edge_ref, field):
    tiles = Tiles(shape)
    rows, depth, halo = tiles.rows, tiles.depth, ITERS
    out_ref[...] = jnp.zeros_like(out_ref)

    def on(upper):
        def one_slice(s, carry):
            for step in range(1, ITERS + 1):
                low, high = (step, rows + ITERS - step) if upper else (step - ITERS, rows - step)
                side, kept = (low - 1, low) if upper else (high, high - 1)

                def read(row):
                    if step > 1:
                        return [field[row + halo, m] for m in range(WAYS)]
                    if 0 <= row < rows:
                        return tiles.load(own_ref, row * depth + s)
                    return tiles.load(core_ref, ((row - rows) if upper else (row + rows)) * depth - (0 if upper else skipped) + s)

                def seen(row):
                    values = read(row)
                    if row == side:
                        for m in range(WAYS):
                            edge_ref[s, step - 1, 0, m] = values[m]
                    return values

                def write(row, here, fresh):
                    if row == kept:
                        for m in range(WAYS):
                            edge_ref[s, step - 1, 1, m] = here[m]
                    if step == ITERS:
                        tiles.store(out_ref, s, row, fresh)
                    else:
                        for m in range(WAYS):
                            field[row + halo, m] = fresh[m]

                tiles.sweep(low, high, seen, write)
            return carry

        lax.fori_loop(0, depth, one_slice, 0)

    core = lax.rem(lax.axis_index("scan"), 2)
    pl.when(core == 0)(lambda: on(True))
    pl.when(core == 1)(lambda: on(False))


def far_kernel(shape, skipped, chip_ref, edge_ref, done_ref, out_ref, field):
    tiles = Tiles(shape)
    rows, depth, halo = tiles.rows, tiles.depth, ITERS
    out_ref[...] = done_ref[...]
    me = lax.axis_index("scan")
    first = jnp.where(me == 0, 0.0, 1.0)
    last = jnp.where(me == lax.axis_size("scan") - 1, 0.0, 1.0)

    def on(upper):
        def one_slice(s, carry):
            for step in range(1, ITERS + 1):
                low, high = (step - ITERS, step) if upper else (rows - step, rows + ITERS - step)
                side, kept = (high - 1, high) if upper else (low, low - 1)

                def read(row):
                    if row == side:
                        return [edge_ref[s, step - 1, 0, m] for m in range(WAYS)]
                    if row == kept:
                        return [edge_ref[s, step - 1, 1, m] for m in range(WAYS)]
                    if step > 1:
                        return [field[row + halo, m] for m in range(WAYS)]
                    return tiles.load(chip_ref, ((row + rows) if upper else (row - rows)) * depth - (skipped if upper else 0) + s)

                def write(row, here, fresh):
                    if step == ITERS:
                        tiles.store(out_ref, s, row, fresh)
                    else:
                        for m in range(WAYS):
                            field[row + halo, m] = fresh[m]

                tiles.sweep(low, high, read, write, [(-1, first)] if upper else [(rows - 1, last)])
            return carry

        lax.fori_loop(0, depth, one_slice, 0)

    core = lax.rem(me, 2)
    pl.when(core == 0)(lambda: on(True))
    pl.when(core == 1)(lambda: on(False))


def copy_kernel(plan, source_ref, *refs):
    count = len(plan)
    sems = refs[count]
    me = lax.axis_index("scan")
    core, y, x = lax.rem(me, 2), lax.rem(me // 2, 2), me // 4
    chips = source_ref.shape[2]
    copies = []
    for out, (theirs, pieces) in zip(refs, plan):
        whose = 1 - core if theirs else core
        for slot, (part, k, e) in enumerate(pieces):
            copies.append(
                pltpu.make_async_copy(
                    source_ref.at[part, :, lax.rem(x + k, chips), 1 - y if e else y, whose],
                    out.at[slot],
                    sems.at[len(copies)],
                )
            )
    for copy in copies:
        copy.start()
    for copy in copies:
        copy.wait()


def copied(split, *plan):
    _, depth, _, _, _, rows, width = split.shape
    moved = 4 * sum(len(pieces) for _, pieces in plan) * depth * rows * width
    return pl.pallas_call(
        lambda *refs: copy_kernel(plan, *refs),
        out_shape=[jax.ShapeDtypeStruct((len(pieces), depth, rows, width), split.dtype) for _, pieces in plan],
        in_specs=[pl.BlockSpec(memory_space=pltpu.HBM)],
        out_specs=[pl.BlockSpec(memory_space=pltpu.VMEM)] * len(plan),
        scratch_shapes=[pltpu.SemaphoreType.DMA((sum(len(pieces) for _, pieces in plan),))],
        cost_estimate=pl.CostEstimate(flops=0, bytes_accessed=moved, transcendentals=0),
        compiler_params=pltpu.CompilerParams(vmem_limit_bytes=moved + 2 * 1024 * 1024),
    )(split)


def on_device(partials, inverses, classes):
    _, parts, depth, rows_total, width = partials.shape
    scans = lax.axis_size("scan")
    cuts = lax.axis_size("cuts")
    rows = rows_total // scans
    lanes = width // cuts
    kinds, total, _ = inverses.shape
    chips = scans // 4
    f32, f16 = jnp.float32, jnp.float16

    def send(array, target, turn=0):
        pairs = [(i, target(i)) for i in range(scans)]
        return lax.ppermute(array, "scan", pairs[turn:] + pairs[:turn])

    def other_core(i):
        return i ^ 1

    def other_y(i):
        return i ^ 2

    def along_x(k):
        return lambda i: (i + 4 * k) % scans

    def paired(own, got):
        return (own.astype(f32) + got.astype(f32)) * SUM_SCALE

    def after(value, made):
        return lax.optimization_barrier((value, made))[0]

    split = partials.reshape(parts, depth, chips, 2, 2, rows, width)
    split = pltpu.with_memory_space_constraint(split, pltpu.HBM)
    early = [(0, 2, 0), (0, 2, 1), (1, 2, 1), (1, 0, 1)]
    late = [(1, 1, 1), (1, 3, 1)] + [(0, k, e) for k in (1, 3, 0) for e in range(2)] + [(1, k, 0) for k in (2, 0, 1, 3)]
    give_early, own_early = copied(split, (True, early), (False, early))
    got_early = send(give_early, other_core)
    give_late, own_late = copied(split, (True, late), (False, late))
    got_late = send(after(give_late, got_early), other_core, 1)

    two_steps = paired(own_early[:2], got_early[:2]).astype(f16)
    y_far = paired(own_early[2:], got_early[2:]).astype(f16)
    came_far = send(y_far, other_y)
    from_left = send(two_steps[0], along_x(1))
    from_right = send(two_steps[1], along_x(3))

    y_near = paired(own_late[:2], got_late[:2]).astype(f16)
    came_near = send(y_near, other_y, 1)
    one_step = paired(own_late[2:6], got_late[2:6])
    mine0 = paired(own_late[6:8], got_late[6:8])
    mine1 = paired(own_late[8:], got_late[8:])

    from_left, from_right = after((from_left, from_right), y_near)
    to_right = jnp.stack([one_step[0] + from_left.astype(f32), one_step[1]]).astype(f16)
    to_left = jnp.stack([one_step[2], one_step[3] + from_right.astype(f32)]).astype(f16)
    x_left = send(to_right, along_x(1))
    x_right = send(to_left, along_x(3))

    came_far = after(came_far, (to_right, to_left))
    far1 = mine1[:2] + came_far.astype(f32)
    two_steps1 = far1[0].astype(f16)
    half = depth // 2
    from_left1 = send(two_steps1[:half], along_x(1), 1)
    from_right1 = send(two_steps1[half:], along_x(3), 1)

    x_left, x_right = after((x_left, x_right), two_steps1)
    over_x = mine0 + x_left.astype(f32) + x_right.astype(f32)
    last = over_x[1].astype(f16)
    part0 = over_x[0] + send(last, other_y, 2).astype(f32)

    came_near, from_left1, from_right1 = after((came_near, from_left1, from_right1), last)
    near1 = mine1[2:] + came_near.astype(f32)
    to_right1 = jnp.concatenate([near1[0, :half] + from_left1.astype(f32), near1[0, half:]]).astype(f16)
    to_left1 = jnp.concatenate([near1[1, :half], near1[1, half:] + from_right1.astype(f32)]).astype(f16)
    x_left1 = send(to_right1, along_x(1), 2)
    x_right1 = send(to_left1, along_x(3), 2)
    part1 = far1[1] + x_left1.astype(f32) + x_right1.astype(f32)

    grad = (jnp.stack([part0, part1]) * (1.0 / SUM_SCALE)).astype(jnp.bfloat16)
    grad = grad.reshape(parts, depth, rows, cuts, lanes).transpose(3, 0, 1, 2, 4)
    weights = after(inverses, last).reshape(kinds, cuts, depth, total).transpose(2, 1, 0, 3).reshape(total, kinds * total)
    upper = lax.axis_index("scan") & 1 == 0
    grad, weights, upper = lax.optimization_barrier((grad, weights, upper))
    grad = lax.all_to_all(grad, "cuts", 0, 0, tiled=True)
    per = rows * parts * depth
    filtered = pl.pallas_call(
        filter_kernel,
        out_shape=jax.ShapeDtypeStruct((cuts * per, lanes), f32),
        scratch_shapes=[pltpu.VMEM((parts, total * rows, lanes), f32)],
        compiler_params=pltpu.CompilerParams(vmem_limit_bytes=16 * 1024 * 1024),
    )(grad, weights, classes)
    coded = (filtered * SCALE).astype(f16).reshape(cuts, per, lanes)
    coded = lax.all_to_all(coded, "cuts", 0, 0, tiled=True)
    coded = coded.reshape(cuts, parts, rows * depth, lanes)
    skipped = (rows - ITERS) * depth // TILE * TILE
    needed = -(-ITERS * depth // TILE) * TILE
    top, bottom = coded[:, :, :needed], coded[:, :, skipped:]
    odds = range(1, scans - 1, 2)
    chip = lax.ppermute(
        jnp.where(upper, top, bottom), "scan", [(i, i + 1) for i in odds] + [(i + 1, i) for i in odds]
    )

    def plain(array):
        return (array.astype(f32) * (1.0 / SCALE)).transpose(1, 0, 2, 3).reshape(-1, lanes)

    middle = plain(coded)
    core = send(after(jnp.where(upper, bottom, top), middle), other_core)
    shape = (cuts, parts, depth, rows, lanes)
    lines = parts * cuts // WAYS
    out = jax.ShapeDtypeStruct((parts * depth, cuts * rows, lanes), f32)
    field = pltpu.VMEM((rows + 2 * ITERS, WAYS, lines, lanes), f32)
    work = cuts * rows * parts * depth * lanes
    done, edges = pl.pallas_call(
        lambda *refs: near_kernel(shape, skipped, *refs),
        out_shape=[out, jax.ShapeDtypeStruct((depth, ITERS, 2, WAYS, lines, lanes), f32)],
        scratch_shapes=[field],
        cost_estimate=pl.CostEstimate(flops=0, bytes_accessed=16 * work, transcendentals=0),
        compiler_params=pltpu.CompilerParams(vmem_limit_bytes=12 * 1024 * 1024),
    )(middle, plain(core))
    chip, edges, done = lax.optimization_barrier((chip, edges, done))
    result = pl.pallas_call(
        lambda *refs: far_kernel(shape, skipped, *refs),
        out_shape=out,
        scratch_shapes=[field],
        compiler_params=pltpu.CompilerParams(vmem_limit_bytes=12 * 1024 * 1024),
    )(plain(chip), edges, done)
    result = result.reshape(parts, depth, cuts, rows, lanes).transpose(0, 1, 3, 2, 4)
    return result.reshape(parts, depth, rows, width)


def solution(mesh):
    placed = (P("scan", None, "cuts", None, None), P(), P("scan", "cuts"))
    return jax.shard_map(
        on_device,
        mesh=mesh,
        in_specs=placed,
        out_specs=P(None, "cuts", "scan", None),
        check_vma=False,
    )
```

```python
import jax
import jax.numpy as jnp
from jax import lax
from jax.experimental import pallas as pl
from jax.experimental.pallas import tpu as pltpu
from jax.sharding import PartitionSpec as P

ITERS = 5
WAYS = 4
MANY = 6
TILE = 16
SUM_SCALE = 1024.0
SCALE = 32.0


def home(lane, shift, lanes):
    return lanes // WAYS * lax.rem(lax.rem(lane, WAYS) + shift, WAYS) + lane // WAYS


def filter_kernel(grad_ref, weights_ref, classes_ref, out_ref, cells):
    blocks, parts, depth, rows, lanes = grad_ref.shape
    total = blocks * depth
    kinds = weights_ref.shape[1] // total
    shift = lax.rem(lax.axis_index("cuts"), WAYS)
    source = lax.broadcasted_iota(jnp.int32, (lanes, lanes), 0)
    target = lax.broadcasted_iota(jnp.int32, (lanes, lanes), 1)
    turn = jnp.where(home(source, shift, lanes) == target, 1.0, 0.0).astype(jnp.bfloat16)
    for part in range(parts):
        flat = grad_ref[:, part].astype(jnp.float32).reshape(total * rows, lanes).astype(jnp.bfloat16)
        cells[part] = jnp.dot(flat, turn, preferred_element_type=jnp.float32)
    labels = jnp.dot(
        classes_ref[...].astype(jnp.float32).astype(jnp.bfloat16), turn, preferred_element_type=jnp.float32
    )
    weights = weights_ref[...]
    for row in range(rows):
        label = jnp.concatenate([labels[row : row + 1, :]] * parts, axis=1)
        values = jnp.concatenate(
            [cells[part, pl.ds(row, total, stride=rows), :] for part in range(parts)], axis=1
        )
        masked = jnp.concatenate(
            [jnp.where(label == float(kind), values, 0.0) for kind in range(kinds)], axis=0
        ).astype(jnp.bfloat16)
        found = jnp.dot(weights, masked, preferred_element_type=jnp.float32)
        for part in range(parts):
            for s in range(depth):
                out_ref[pl.ds((part * rows + row) * depth + s, blocks, stride=rows * parts * depth), :] = found[
                    s * blocks : (s + 1) * blocks, part * lanes : (part + 1) * lanes
                ]


class Tiles:
    def __init__(self, shape):
        self.blocks, self.parts, self.depth, self.rows, self.lanes = shape
        self.groups = self.blocks // WAYS
        self.lines = self.parts * self.groups
        self.size = self.lanes // WAYS
        self.lane = lax.broadcasted_iota(jnp.int32, (self.lines, self.lanes), 1)
        line = lax.broadcasted_iota(jnp.int32, (self.lines, self.lanes), 0)
        self.at_left = self.lane == 0
        self.at_right = self.lane == self.lanes - 1
        self.inner = jnp.where(self.at_right & (lax.rem(line, self.groups) == self.groups - 1), 0.0, 1.0)

    def skewed(self, values):
        found = []
        for m in range(WAYS):
            pick = values[-m % WAYS]
            for group in range(1, WAYS):
                pick = jnp.where(self.lane // self.size == group, values[(group - m) % WAYS], pick)
            found.append(pick)
        return found

    def load(self, source, at):
        per = source.shape[0] // (self.blocks * self.parts)
        found = [source[pl.ds(b * per + at, self.lines, stride=WAYS * per), :] for b in range(WAYS)]
        return [
            pltpu.roll(f, (self.lanes - self.size * m) % self.lanes, 1) for m, f in enumerate(self.skewed(found))
        ]

    def store(self, out_ref, s, row, values):
        values = self.skewed([pltpu.roll(v, self.size * m, 1) for m, v in enumerate(values)])
        for b in range(WAYS):
            value = jnp.take_along_axis(values[b], home(self.lane, b, self.lanes), axis=1)
            for part in range(self.parts):
                out_ref[part * self.depth + s, pl.ds(b * self.rows + row, self.groups, stride=WAYS * self.rows), :] = (
                    value[part * self.groups : (part + 1) * self.groups]
                )

    def sweep(self, count, read, write, scale=None):
        before = None
        here = read(-1)
        for row in range(-1, count):
            below = read(row + 1)
            down = [b - h for b, h in zip(below, here)]
            if scale is not None:
                down = [d * scale(row) for d in down]
            near = pltpu.roll(here[0], self.lanes - 1, 1)
            near = jnp.where(self.at_right, pltpu.roll(near, self.lines - 1, 0), near)
            across = [n - h for n, h in zip(here[1:] + [near], here)]
            across[-1] = across[-1] * self.inner
            power = [d * d + a * a for d, a in zip(down, across)]
            inverse = [lax.rsqrt(p + pltpu.roll(p, self.groups, 0) + 1.0) for p in power]
            flux = [d * i for d, i in zip(down, inverse)]
            if before is not None:
                sides = [a * i for a, i in zip(across, inverse)]
                near = pltpu.roll(sides[-1], 1, 1)
                near = jnp.where(self.at_left, pltpu.roll(near, 1, 0), near)
                fresh = [
                    h + 0.2 * (f - b + s1 - s0)
                    for h, f, b, s1, s0 in zip(here, flux, before, sides, [near] + sides[:-1])
                ]
                write(row, fresh)
            before = flux
            here = below


def read_row(ref, *at):
    return [ref[(*at, m)] for m in range(WAYS)]


def write_row(ref, values, *at):
    for m in range(WAYS):
        ref[(*at, m)] = values[m]


def near_kernel(shape, skipped, own_ref, core_ref, out_ref, edge_ref, field):
    tiles = Tiles(shape)
    rows, depth, halo = tiles.rows, tiles.depth, ITERS
    upper = lax.rem(lax.axis_index("scan"), 2) == 0
    out_ref[...] = jnp.zeros_like(out_ref)

    def one_slice(s, carry):
        for row in range(rows):
            write_row(field, tiles.load(own_ref, row * depth + s), row + halo)
        for row in range(halo):
            at = jnp.where(upper, row * depth, (row + rows - halo) * depth - skipped)
            write_row(field, tiles.load(core_ref, at + s), jnp.where(upper, rows + halo, 0) + row)
        for step in range(1, ITERS + 1):
            low = jnp.where(upper, step, step - ITERS) + halo
            count = rows + ITERS - 2 * step
            side = jnp.where(upper, low - 1, low + count)
            kept = jnp.where(upper, low, low + count - 1)
            write_row(edge_ref, read_row(field, side), s, step - 1, 0)
            write_row(edge_ref, read_row(field, kept), s, step - 1, 1)
            tiles.sweep(
                count,
                lambda row, low=low: read_row(field, low + row),
                lambda row, fresh, low=low: write_row(field, fresh, low + row),
            )
        for row in range(rows - ITERS):
            at = jnp.where(upper, ITERS, 0) + row
            tiles.store(out_ref, s, at, read_row(field, at + halo))
        return carry

    lax.fori_loop(0, depth, one_slice, 0)


def far_kernel(shape, skipped, chip_ref, edge_ref, done_ref, out_ref, field):
    tiles = Tiles(shape)
    rows, depth, halo = tiles.rows, tiles.depth, ITERS
    many = field.shape[0]
    me = lax.axis_index("scan")
    upper = lax.rem(me, 2) == 0
    stop = jnp.where(me == 0, halo - 1, jnp.where(me == lax.axis_size("scan") - 1, halo + rows - 1, -1))
    out_ref[...] = done_ref[...]

    def some_slices(group, carry):
        for i in range(many):
            for row in range(halo):
                at = jnp.where(upper, (row + rows - halo) * depth - skipped, row * depth)
                write_row(
                    field, tiles.load(chip_ref, at + group * many + i), i, jnp.where(upper, 0, rows + halo) + row
                )

        def one_step(step, carry):
            low = jnp.where(upper, step - ITERS, rows - step) + halo
            side = jnp.where(upper, low + ITERS - 1, low)
            kept = jnp.where(upper, low + ITERS, low - 1)
            for i in range(many):
                s = group * many + i
                write_row(field, read_row(edge_ref, s, step - 1, 0), i, side)
                write_row(field, read_row(edge_ref, s, step - 1, 1), i, kept)
            for i in range(many):
                tiles.sweep(
                    ITERS,
                    lambda row, i=i: read_row(field, i, low + row),
                    lambda row, fresh, i=i: write_row(field, fresh, i, low + row),
                    lambda row: jnp.where(low + row == stop, 0.0, 1.0),
                )
            return carry

        lax.fori_loop(1, ITERS + 1, one_step, 0)

        def one_row(row, carry):
            at = jnp.where(upper, 0, rows - ITERS) + row
            for i in range(many):
                tiles.store(out_ref, group * many + i, at, read_row(field, i, at + halo))
            return carry

        lax.fori_loop(0, ITERS, one_row, 0)
        return carry

    lax.fori_loop(0, depth // many, some_slices, 0)


def copy_kernel(plan, source_ref, *refs):
    count = len(plan)
    sems = refs[count]
    me = lax.axis_index("scan")
    core, y, x = lax.rem(me, 2), lax.rem(me // 2, 2), me // 4
    chips = source_ref.shape[2]
    copies = []
    for out, (theirs, pieces) in zip(refs, plan):
        whose = 1 - core if theirs else core
        for slot, (part, k, e) in enumerate(pieces):
            copies.append(
                pltpu.make_async_copy(
                    source_ref.at[part, :, lax.rem(x + k, chips), 1 - y if e else y, whose],
                    out.at[slot],
                    sems.at[len(copies)],
                )
            )
    for copy in copies:
        copy.start()
    for copy in copies:
        copy.wait()


def copied(split, *plan):
    _, depth, _, _, _, rows, width = split.shape
    moved = 4 * sum(len(pieces) for _, pieces in plan) * depth * rows * width
    return pl.pallas_call(
        lambda *refs: copy_kernel(plan, *refs),
        out_shape=[jax.ShapeDtypeStruct((len(pieces), depth, rows, width), split.dtype) for _, pieces in plan],
        in_specs=[pl.BlockSpec(memory_space=pltpu.HBM)],
        out_specs=[pl.BlockSpec(memory_space=pltpu.VMEM)] * len(plan),
        scratch_shapes=[pltpu.SemaphoreType.DMA((sum(len(pieces) for _, pieces in plan),))],
        cost_estimate=pl.CostEstimate(flops=0, bytes_accessed=moved, transcendentals=0),
        compiler_params=pltpu.CompilerParams(vmem_limit_bytes=moved + 2 * 1024 * 1024),
    )(split)


def on_device(partials, inverses, classes):
    _, parts, depth, rows_total, width = partials.shape
    scans = lax.axis_size("scan")
    cuts = lax.axis_size("cuts")
    rows = rows_total // scans
    lanes = width // cuts
    kinds, total, _ = inverses.shape
    chips = scans // 4
    f32, f16 = jnp.float32, jnp.float16

    def send(array, target, turn=0):
        pairs = [(i, target(i)) for i in range(scans)]
        return lax.ppermute(array, "scan", pairs[turn:] + pairs[:turn])

    def other_core(i):
        return i ^ 1

    def other_y(i):
        return i ^ 2

    def along_x(k):
        return lambda i: (i + 4 * k) % scans

    def paired(own, got):
        return (own.astype(f32) + got.astype(f32)) * SUM_SCALE

    def after(value, made):
        return lax.optimization_barrier((value, made))[0]

    split = partials.reshape(parts, depth, chips, 2, 2, rows, width)
    split = pltpu.with_memory_space_constraint(split, pltpu.HBM)
    early = [(0, 2, 0), (0, 2, 1), (1, 2, 1), (1, 0, 1)]
    late = [(1, 1, 1), (1, 3, 1)] + [(0, k, e) for k in (1, 3, 0) for e in range(2)] + [(1, k, 0) for k in (2, 0, 1, 3)]
    give_early, own_early = copied(split, (True, early), (False, early))
    got_early = send(give_early, other_core)
    give_late, own_late = copied(split, (True, late), (False, late))
    got_late = send(after(give_late, got_early), other_core, 1)

    two_steps = paired(own_early[:2], got_early[:2]).astype(f16)
    y_far = paired(own_early[2:], got_early[2:]).astype(f16)
    came_far = send(y_far, other_y)
    from_left = send(two_steps[0], along_x(1))
    from_right = send(two_steps[1], along_x(3))

    y_near = paired(own_late[:2], got_late[:2]).astype(f16)
    came_near = send(y_near, other_y, 1)
    one_step = paired(own_late[2:6], got_late[2:6])
    mine0 = paired(own_late[6:8], got_late[6:8])
    mine1 = paired(own_late[8:], got_late[8:])

    from_left, from_right = after((from_left, from_right), y_near)
    to_right = jnp.stack([one_step[0] + from_left.astype(f32), one_step[1]]).astype(f16)
    to_left = jnp.stack([one_step[2], one_step[3] + from_right.astype(f32)]).astype(f16)
    x_left = send(to_right, along_x(1))
    x_right = send(to_left, along_x(3))

    came_far = after(came_far, (to_right, to_left))
    far1 = mine1[:2] + came_far.astype(f32)
    two_steps1 = far1[0].astype(f16)
    half = depth // 2
    from_left1 = send(two_steps1[:half], along_x(1), 1)
    from_right1 = send(two_steps1[half:], along_x(3), 1)

    x_left, x_right = after((x_left, x_right), two_steps1)
    over_x = mine0 + x_left.astype(f32) + x_right.astype(f32)
    last = over_x[1].astype(f16)
    part0 = over_x[0] + send(last, other_y, 2).astype(f32)

    came_near, from_left1, from_right1 = after((came_near, from_left1, from_right1), last)
    near1 = mine1[2:] + came_near.astype(f32)
    to_right1 = jnp.concatenate([near1[0, :half] + from_left1.astype(f32), near1[0, half:]]).astype(f16)
    to_left1 = jnp.concatenate([near1[1, :half], near1[1, half:] + from_right1.astype(f32)]).astype(f16)
    x_left1 = send(to_right1, along_x(1), 2)
    x_right1 = send(to_left1, along_x(3), 2)
    part1 = far1[1] + x_left1.astype(f32) + x_right1.astype(f32)

    grad = (jnp.stack([part0, part1]) * (1.0 / SUM_SCALE)).astype(jnp.bfloat16)
    grad = grad.reshape(parts, depth, rows, cuts, lanes).transpose(3, 0, 1, 2, 4)
    weights = after(inverses, last).reshape(kinds, cuts, depth, total).transpose(2, 1, 0, 3).reshape(total, kinds * total)
    upper = lax.axis_index("scan") & 1 == 0
    grad, weights, upper = lax.optimization_barrier((grad, weights, upper))
    grad = lax.all_to_all(grad, "cuts", 0, 0, tiled=True)
    per = rows * parts * depth
    filtered = pl.pallas_call(
        filter_kernel,
        out_shape=jax.ShapeDtypeStruct((cuts * per, lanes), f32),
        scratch_shapes=[pltpu.VMEM((parts, total * rows, lanes), f32)],
        compiler_params=pltpu.CompilerParams(vmem_limit_bytes=16 * 1024 * 1024),
    )(grad, weights, classes)
    coded = (filtered * SCALE).astype(f16).reshape(cuts, per, lanes)
    coded = lax.all_to_all(coded, "cuts", 0, 0, tiled=True)
    coded = coded.reshape(cuts, parts, rows * depth, lanes)
    skipped = (rows - ITERS) * depth // TILE * TILE
    needed = -(-ITERS * depth // TILE) * TILE
    top, bottom = coded[:, :, :needed], coded[:, :, skipped:]
    odds = range(1, scans - 1, 2)
    chip = lax.ppermute(
        jnp.where(upper, top, bottom), "scan", [(i, i + 1) for i in odds] + [(i + 1, i) for i in odds]
    )

    def plain(array):
        return (array.astype(f32) * (1.0 / SCALE)).transpose(1, 0, 2, 3).reshape(-1, lanes)

    middle = plain(coded)
    core = send(after(jnp.where(upper, bottom, top), middle), other_core)
    shape = (cuts, parts, depth, rows, lanes)
    lines = parts * cuts // WAYS
    out = jax.ShapeDtypeStruct((parts * depth, cuts * rows, lanes), f32)
    field = pltpu.VMEM((rows + 2 * ITERS, WAYS, lines, lanes), f32)
    work = cuts * rows * parts * depth * lanes
    done, edges = pl.pallas_call(
        lambda *refs: near_kernel(shape, skipped, *refs),
        out_shape=[out, jax.ShapeDtypeStruct((depth, ITERS, 2, WAYS, lines, lanes), f32)],
        scratch_shapes=[field],
        cost_estimate=pl.CostEstimate(flops=0, bytes_accessed=16 * work, transcendentals=0),
        compiler_params=pltpu.CompilerParams(vmem_limit_bytes=12 * 1024 * 1024),
    )(middle, plain(core))
    chip, edges, done = lax.optimization_barrier((chip, edges, done))
    result = pl.pallas_call(
        lambda *refs: far_kernel(shape, skipped, *refs),
        out_shape=out,
        scratch_shapes=[pltpu.VMEM((MANY, rows + 2 * ITERS, WAYS, lines, lanes), f32)],
        compiler_params=pltpu.CompilerParams(vmem_limit_bytes=12 * 1024 * 1024),
    )(plain(chip), edges, done)
    result = result.reshape(parts, depth, cuts, rows, lanes).transpose(0, 1, 3, 2, 4)
    return result.reshape(parts, depth, rows, width)


def solution(mesh):
    placed = (P("scan", None, "cuts", None, None), P(), P("scan", "cuts"))
    return jax.shard_map(
        on_device,
        mesh=mesh,
        in_specs=placed,
        out_specs=P(None, "cuts", "scan", None),
        check_vma=False,
    )
```

```python
import jax
import jax.numpy as jnp
from jax import lax
from jax.experimental import pallas as pl
from jax.experimental.pallas import tpu as pltpu
from jax.sharding import PartitionSpec as P

ITERS = 5
WAYS = 4
MANY = 6
TILE = 16
SUM_SCALE = 1024.0
SCALE = 32.0


def home(lane, shift, lanes):
    return lanes // WAYS * lax.rem(lax.rem(lane, WAYS) + shift, WAYS) + lane // WAYS


def filter_kernel(grad_ref, weights_ref, classes_ref, out_ref, cells):
    blocks, parts, depth, rows, lanes = grad_ref.shape
    total = blocks * depth
    kinds = weights_ref.shape[1] // total
    shift = lax.rem(lax.axis_index("cuts"), WAYS)
    source = lax.broadcasted_iota(jnp.int32, (lanes, lanes), 0)
    target = lax.broadcasted_iota(jnp.int32, (lanes, lanes), 1)
    turn = jnp.where(home(source, shift, lanes) == target, 1.0, 0.0).astype(jnp.bfloat16)
    for part in range(parts):
        flat = grad_ref[:, part].astype(jnp.float32).reshape(total * rows, lanes).astype(jnp.bfloat16)
        cells[part] = jnp.dot(flat, turn, preferred_element_type=jnp.float32)
    labels = jnp.dot(
        classes_ref[...].astype(jnp.float32).astype(jnp.bfloat16), turn, preferred_element_type=jnp.float32
    )
    weights = weights_ref[...]
    for row in range(rows):
        label = jnp.concatenate([labels[row : row + 1, :]] * parts, axis=1)
        values = jnp.concatenate(
            [cells[part, pl.ds(row, total, stride=rows), :] for part in range(parts)], axis=1
        )
        masked = jnp.concatenate(
            [jnp.where(label == float(kind), values, 0.0) for kind in range(kinds)], axis=0
        ).astype(jnp.bfloat16)
        found = jnp.dot(weights, masked, preferred_element_type=jnp.float32)
        for part in range(parts):
            for s in range(depth):
                out_ref[pl.ds((part * rows + row) * depth + s, blocks, stride=rows * parts * depth), :] = found[
                    s * blocks : (s + 1) * blocks, part * lanes : (part + 1) * lanes
                ]


class Tiles:
    def __init__(self, shape):
        self.blocks, self.parts, self.depth, self.rows, self.lanes = shape
        self.groups = self.blocks // WAYS
        self.lines = self.parts * self.groups
        self.size = self.lanes // WAYS
        self.lane = lax.broadcasted_iota(jnp.int32, (self.lines, self.lanes), 1)
        line = lax.broadcasted_iota(jnp.int32, (self.lines, self.lanes), 0)
        self.at_left = self.lane == 0
        self.at_right = self.lane == self.lanes - 1
        self.inner = jnp.where(self.at_right & (lax.rem(line, self.groups) == self.groups - 1), 0.0, 1.0)

    def skewed(self, values):
        found = []
        for m in range(WAYS):
            pick = values[-m % WAYS]
            for group in range(1, WAYS):
                pick = jnp.where(self.lane // self.size == group, values[(group - m) % WAYS], pick)
            found.append(pick)
        return found

    def load(self, source, at):
        per = source.shape[0] // (self.blocks * self.parts)
        found = [source[pl.ds(b * per + at, self.lines, stride=WAYS * per), :] for b in range(WAYS)]
        return [
            pltpu.roll(f, (self.lanes - self.size * m) % self.lanes, 1) for m, f in enumerate(self.skewed(found))
        ]

    def store(self, out_ref, s, row, values):
        values = self.skewed([pltpu.roll(v, self.size * m, 1) for m, v in enumerate(values)])
        for b in range(WAYS):
            value = jnp.take_along_axis(values[b], home(self.lane, b, self.lanes), axis=1)
            for part in range(self.parts):
                out_ref[part * self.depth + s, pl.ds(b * self.rows + row, self.groups, stride=WAYS * self.rows), :] = (
                    value[part * self.groups : (part + 1) * self.groups]
                )

    def sweep(self, low, high, read, write, scale=None):
        before = None
        here = read(low - 1)
        for row in range(low - 1, high):
            below = read(row + 1)
            down = [b - h for b, h in zip(below, here)]
            if scale is not None:
                down = [d * scale(row) for d in down]
            near = pltpu.roll(here[0], self.lanes - 1, 1)
            near = jnp.where(self.at_right, pltpu.roll(near, self.lines - 1, 0), near)
            across = [n - h for n, h in zip(here[1:] + [near], here)]
            across[-1] = across[-1] * self.inner
            power = [d * d + a * a for d, a in zip(down, across)]
            inverse = [lax.rsqrt(p + pltpu.roll(p, self.groups, 0) + 1.0) for p in power]
            flux = [d * i for d, i in zip(down, inverse)]
            if before is not None:
                sides = [a * i for a, i in zip(across, inverse)]
                near = pltpu.roll(sides[-1], 1, 1)
                near = jnp.where(self.at_left, pltpu.roll(near, 1, 0), near)
                fresh = [
                    h + 0.2 * (f - b + s1 - s0)
                    for h, f, b, s1, s0 in zip(here, flux, before, sides, [near] + sides[:-1])
                ]
                write(row, here, fresh)
            before = flux
            here = below


def read_row(ref, *at):
    return [ref[(*at, m)] for m in range(WAYS)]


def write_row(ref, values, *at):
    for m in range(WAYS):
        ref[(*at, m)] = values[m]


def near_kernel(shape, skipped, own_ref, core_ref, out_ref, edge_ref, field):
    tiles = Tiles(shape)
    rows, depth, halo = tiles.rows, tiles.depth, ITERS
    out_ref[...] = jnp.zeros_like(out_ref)

    def on(upper):
        def one_slice(s, carry):
            for step in range(1, ITERS + 1):
                low, high = (step, rows + ITERS - step) if upper else (step - ITERS, rows - step)
                side, kept = (low - 1, low) if upper else (high, high - 1)

                def read(row):
                    if step > 1:
                        return [field[row + halo, m] for m in range(WAYS)]
                    if 0 <= row < rows:
                        return tiles.load(own_ref, row * depth + s)
                    return tiles.load(core_ref, ((row - rows) if upper else (row + rows)) * depth - (0 if upper else skipped) + s)

                def seen(row):
                    values = read(row)
                    if row == side:
                        for m in range(WAYS):
                            edge_ref[s, step - 1, 0, m] = values[m]
                    return values

                def write(row, here, fresh):
                    if row == kept:
                        for m in range(WAYS):
                            edge_ref[s, step - 1, 1, m] = here[m]
                    if step == ITERS:
                        tiles.store(out_ref, s, row, fresh)
                    else:
                        for m in range(WAYS):
                            field[row + halo, m] = fresh[m]

                tiles.sweep(low, high, seen, write)
            return carry

        lax.fori_loop(0, depth, one_slice, 0)

    core = lax.rem(lax.axis_index("scan"), 2)
    pl.when(core == 0)(lambda: on(True))
    pl.when(core == 1)(lambda: on(False))


def far_kernel(shape, skipped, chip_ref, edge_ref, done_ref, out_ref, field):
    tiles = Tiles(shape)
    rows, depth, halo = tiles.rows, tiles.depth, ITERS
    many = field.shape[0]
    me = lax.axis_index("scan")
    upper = lax.rem(me, 2) == 0
    stop = jnp.where(me == 0, halo - 1, jnp.where(me == lax.axis_size("scan") - 1, halo + rows - 1, -1))
    out_ref[...] = done_ref[...]

    def some_slices(group, carry):
        for i in range(many):
            for row in range(halo):
                at = jnp.where(upper, (row + rows - halo) * depth - skipped, row * depth)
                write_row(
                    field, tiles.load(chip_ref, at + group * many + i), i, jnp.where(upper, 0, rows + halo) + row
                )

        def one_step(step, carry):
            low = jnp.where(upper, step - ITERS, rows - step) + halo
            side = jnp.where(upper, low + ITERS - 1, low)
            kept = jnp.where(upper, low + ITERS, low - 1)
            for i in range(many):
                s = group * many + i
                write_row(field, read_row(edge_ref, s, step - 1, 0), i, side)
                write_row(field, read_row(edge_ref, s, step - 1, 1), i, kept)
            for i in range(many):
                tiles.sweep(
                    0,
                    ITERS,
                    lambda row, i=i: read_row(field, i, low + row),
                    lambda row, here, fresh, i=i: write_row(field, fresh, i, low + row),
                    lambda row: jnp.where(low + row == stop, 0.0, 1.0),
                )
            return carry

        lax.fori_loop(1, ITERS + 1, one_step, 0)

        def one_row(row, carry):
            at = jnp.where(upper, 0, rows - ITERS) + row
            for i in range(many):
                tiles.store(out_ref, group * many + i, at, read_row(field, i, at + halo))
            return carry

        lax.fori_loop(0, ITERS, one_row, 0)
        return carry

    lax.fori_loop(0, depth // many, some_slices, 0)


def copy_kernel(plan, source_ref, *refs):
    count = len(plan)
    sems = refs[count]
    me = lax.axis_index("scan")
    core, y, x = lax.rem(me, 2), lax.rem(me // 2, 2), me // 4
    chips = source_ref.shape[2]
    copies = []
    for out, (theirs, pieces) in zip(refs, plan):
        whose = 1 - core if theirs else core
        for slot, (part, k, e) in enumerate(pieces):
            copies.append(
                pltpu.make_async_copy(
                    source_ref.at[part, :, lax.rem(x + k, chips), 1 - y if e else y, whose],
                    out.at[slot],
                    sems.at[len(copies)],
                )
            )
    for copy in copies:
        copy.start()
    for copy in copies:
        copy.wait()


def copied(split, *plan):
    _, depth, _, _, _, rows, width = split.shape
    moved = 4 * sum(len(pieces) for _, pieces in plan) * depth * rows * width
    return pl.pallas_call(
        lambda *refs: copy_kernel(plan, *refs),
        out_shape=[jax.ShapeDtypeStruct((len(pieces), depth, rows, width), split.dtype) for _, pieces in plan],
        in_specs=[pl.BlockSpec(memory_space=pltpu.HBM)],
        out_specs=[pl.BlockSpec(memory_space=pltpu.VMEM)] * len(plan),
        scratch_shapes=[pltpu.SemaphoreType.DMA((sum(len(pieces) for _, pieces in plan),))],
        cost_estimate=pl.CostEstimate(flops=0, bytes_accessed=moved, transcendentals=0),
        compiler_params=pltpu.CompilerParams(vmem_limit_bytes=moved + 2 * 1024 * 1024),
    )(split)


def on_device(partials, inverses, classes):
    _, parts, depth, rows_total, width = partials.shape
    scans = lax.axis_size("scan")
    cuts = lax.axis_size("cuts")
    rows = rows_total // scans
    lanes = width // cuts
    kinds, total, _ = inverses.shape
    chips = scans // 4
    f32, f16 = jnp.float32, jnp.float16

    def send(array, target, turn=0):
        pairs = [(i, target(i)) for i in range(scans)]
        return lax.ppermute(array, "scan", pairs[turn:] + pairs[:turn])

    def other_core(i):
        return i ^ 1

    def other_y(i):
        return i ^ 2

    def along_x(k):
        return lambda i: (i + 4 * k) % scans

    def paired(own, got):
        return (own.astype(f32) + got.astype(f32)) * SUM_SCALE

    def after(value, made):
        return lax.optimization_barrier((value, made))[0]

    split = partials.reshape(parts, depth, chips, 2, 2, rows, width)
    split = pltpu.with_memory_space_constraint(split, pltpu.HBM)
    early = [(0, 2, 0), (0, 2, 1), (1, 2, 1), (1, 0, 1)]
    late = [(1, 1, 1), (1, 3, 1)] + [(0, k, e) for k in (1, 3, 0) for e in range(2)] + [(1, k, 0) for k in (2, 0, 1, 3)]
    give_early, own_early = copied(split, (True, early), (False, early))
    got_early = send(give_early, other_core)
    give_late, own_late = copied(split, (True, late), (False, late))
    got_late = send(after(give_late, got_early), other_core, 1)

    two_steps = paired(own_early[:2], got_early[:2]).astype(f16)
    y_far = paired(own_early[2:], got_early[2:]).astype(f16)
    came_far = send(y_far, other_y)
    from_left = send(two_steps[0], along_x(1))
    from_right = send(two_steps[1], along_x(3))

    y_near = paired(own_late[:2], got_late[:2]).astype(f16)
    came_near = send(y_near, other_y, 1)
    one_step = paired(own_late[2:6], got_late[2:6])
    mine0 = paired(own_late[6:8], got_late[6:8])
    mine1 = paired(own_late[8:], got_late[8:])

    from_left, from_right = after((from_left, from_right), y_near)
    to_right = jnp.stack([one_step[0] + from_left.astype(f32), one_step[1]]).astype(f16)
    to_left = jnp.stack([one_step[2], one_step[3] + from_right.astype(f32)]).astype(f16)
    x_left = send(to_right, along_x(1))
    x_right = send(to_left, along_x(3))

    came_far = after(came_far, (to_right, to_left))
    far1 = mine1[:2] + came_far.astype(f32)
    two_steps1 = far1[0].astype(f16)
    half = depth // 2
    from_left1 = send(two_steps1[:half], along_x(1), 1)
    from_right1 = send(two_steps1[half:], along_x(3), 1)

    x_left, x_right = after((x_left, x_right), two_steps1)
    over_x = mine0 + x_left.astype(f32) + x_right.astype(f32)
    last = over_x[1].astype(f16)
    part0 = over_x[0] + send(last, other_y, 2).astype(f32)

    came_near, from_left1, from_right1 = after((came_near, from_left1, from_right1), last)
    near1 = mine1[2:] + came_near.astype(f32)
    to_right1 = jnp.concatenate([near1[0, :half] + from_left1.astype(f32), near1[0, half:]]).astype(f16)
    to_left1 = jnp.concatenate([near1[1, :half], near1[1, half:] + from_right1.astype(f32)]).astype(f16)
    x_left1 = send(to_right1, along_x(1), 2)
    x_right1 = send(to_left1, along_x(3), 2)
    part1 = far1[1] + x_left1.astype(f32) + x_right1.astype(f32)

    grad = (jnp.stack([part0, part1]) * (1.0 / SUM_SCALE)).astype(jnp.bfloat16)
    grad = grad.reshape(parts, depth, rows, cuts, lanes).transpose(3, 0, 1, 2, 4)
    weights = after(inverses, last).reshape(kinds, cuts, depth, total).transpose(2, 1, 0, 3).reshape(total, kinds * total)
    upper = lax.axis_index("scan") & 1 == 0
    grad, weights, upper = lax.optimization_barrier((grad, weights, upper))
    grad = lax.all_to_all(grad, "cuts", 0, 0, tiled=True)
    per = rows * parts * depth
    filtered = pl.pallas_call(
        filter_kernel,
        out_shape=jax.ShapeDtypeStruct((cuts * per, lanes), f32),
        scratch_shapes=[pltpu.VMEM((parts, total * rows, lanes), f32)],
        compiler_params=pltpu.CompilerParams(vmem_limit_bytes=16 * 1024 * 1024),
    )(grad, weights, classes)
    coded = (filtered * SCALE).astype(f16).reshape(cuts, per, lanes)
    coded = lax.all_to_all(coded, "cuts", 0, 0, tiled=True)
    coded = coded.reshape(cuts, parts, rows * depth, lanes)
    skipped = (rows - ITERS) * depth // TILE * TILE
    needed = -(-ITERS * depth // TILE) * TILE
    top, bottom = coded[:, :, :needed], coded[:, :, skipped:]
    odds = range(1, scans - 1, 2)
    chip = lax.ppermute(
        jnp.where(upper, top, bottom), "scan", [(i, i + 1) for i in odds] + [(i + 1, i) for i in odds]
    )

    def plain(array):
        return (array.astype(f32) * (1.0 / SCALE)).transpose(1, 0, 2, 3).reshape(-1, lanes)

    middle = plain(coded)
    core = send(after(jnp.where(upper, bottom, top), middle), other_core)
    shape = (cuts, parts, depth, rows, lanes)
    lines = parts * cuts // WAYS
    out = jax.ShapeDtypeStruct((parts * depth, cuts * rows, lanes), f32)
    field = pltpu.VMEM((rows + 2 * ITERS, WAYS, lines, lanes), f32)
    work = cuts * rows * parts * depth * lanes
    done, edges = pl.pallas_call(
        lambda *refs: near_kernel(shape, skipped, *refs),
        out_shape=[out, jax.ShapeDtypeStruct((depth, ITERS, 2, WAYS, lines, lanes), f32)],
        scratch_shapes=[field],
        cost_estimate=pl.CostEstimate(flops=0, bytes_accessed=16 * work, transcendentals=0),
        compiler_params=pltpu.CompilerParams(vmem_limit_bytes=12 * 1024 * 1024),
    )(middle, plain(core))
    chip, edges, done = lax.optimization_barrier((chip, edges, done))
    result = pl.pallas_call(
        lambda *refs: far_kernel(shape, skipped, *refs),
        out_shape=out,
        scratch_shapes=[pltpu.VMEM((MANY, rows + 2 * ITERS, WAYS, lines, lanes), f32)],
        compiler_params=pltpu.CompilerParams(vmem_limit_bytes=12 * 1024 * 1024),
    )(plain(chip), edges, done)
    result = result.reshape(parts, depth, cuts, rows, lanes).transpose(0, 1, 3, 2, 4)
    return result.reshape(parts, depth, rows, width)


def solution(mesh):
    placed = (P("scan", None, "cuts", None, None), P(), P("scan", "cuts"))
    return jax.shard_map(
        on_device,
        mesh=mesh,
        in_specs=placed,
        out_specs=P(None, "cuts", "scan", None),
        check_vma=False,
    )
```

```python
import jax
import jax.numpy as jnp
from jax import lax
from jax.experimental import pallas as pl
from jax.experimental.pallas import tpu as pltpu
from jax.sharding import PartitionSpec as P

ITERS = 5
WAYS = 4
MANY = 6
TILE = 16
SUM_SCALE = 1024.0
SCALE = 32.0


def home(lane, shift, lanes):
    return lanes // WAYS * lax.rem(lax.rem(lane, WAYS) + shift, WAYS) + lane // WAYS


def filter_kernel(grad_ref, weights_ref, classes_ref, out_ref, cells):
    blocks, parts, depth, rows, lanes = grad_ref.shape
    total = blocks * depth
    kinds = weights_ref.shape[1] // total
    shift = lax.rem(lax.axis_index("cuts"), WAYS)
    source = lax.broadcasted_iota(jnp.int32, (lanes, lanes), 0)
    target = lax.broadcasted_iota(jnp.int32, (lanes, lanes), 1)
    turn = jnp.where(home(source, shift, lanes) == target, 1.0, 0.0).astype(jnp.bfloat16)
    for part in range(parts):
        flat = grad_ref[:, part].astype(jnp.float32).reshape(total * rows, lanes).astype(jnp.bfloat16)
        cells[part] = jnp.dot(flat, turn, preferred_element_type=jnp.float32)
    labels = jnp.dot(
        classes_ref[...].astype(jnp.float32).astype(jnp.bfloat16), turn, preferred_element_type=jnp.float32
    )
    weights = weights_ref[...]
    for row in range(rows):
        label = jnp.concatenate([labels[row : row + 1, :]] * parts, axis=1)
        values = jnp.concatenate(
            [cells[part, pl.ds(row, total, stride=rows), :] for part in range(parts)], axis=1
        )
        masked = jnp.concatenate(
            [jnp.where(label == float(kind), values, 0.0) for kind in range(kinds)], axis=0
        ).astype(jnp.bfloat16)
        found = jnp.dot(weights, masked, preferred_element_type=jnp.float32)
        for part in range(parts):
            for s in range(depth):
                out_ref[pl.ds((part * rows + row) * depth + s, blocks, stride=rows * parts * depth), :] = found[
                    s * blocks : (s + 1) * blocks, part * lanes : (part + 1) * lanes
                ]


class Tiles:
    def __init__(self, shape):
        self.blocks, self.parts, self.depth, self.rows, self.lanes = shape
        self.groups = self.blocks // WAYS
        self.lines = self.parts * self.groups
        self.size = self.lanes // WAYS
        self.lane = lax.broadcasted_iota(jnp.int32, (self.lines, self.lanes), 1)
        line = lax.broadcasted_iota(jnp.int32, (self.lines, self.lanes), 0)
        self.at_left = self.lane == 0
        self.homes = [home(self.lane, b, self.lanes) for b in range(WAYS)]
        self.at_right = self.lane == self.lanes - 1
        self.inner = jnp.where(self.at_right & (lax.rem(line, self.groups) == self.groups - 1), 0.0, 1.0)

    def skewed(self, values):
        found = []
        for m in range(WAYS):
            pick = values[-m % WAYS]
            for group in range(1, WAYS):
                pick = jnp.where(self.lane // self.size == group, values[(group - m) % WAYS], pick)
            found.append(pick)
        return found

    def load(self, source, at):
        per = source.shape[0] // (self.blocks * self.parts)
        found = [source[pl.ds(b * per + at, self.lines, stride=WAYS * per), :] for b in range(WAYS)]
        return [
            pltpu.roll(f, (self.lanes - self.size * m) % self.lanes, 1) for m, f in enumerate(self.skewed(found))
        ]

    def store(self, out_ref, s, row, values):
        values = self.skewed([pltpu.roll(v, self.size * m, 1) for m, v in enumerate(values)])
        for b in range(WAYS):
            value = jnp.take_along_axis(values[b], self.homes[b], axis=1)
            for part in range(self.parts):
                out_ref[part * self.depth + s, pl.ds(b * self.rows + row, self.groups, stride=WAYS * self.rows), :] = (
                    value[part * self.groups : (part + 1) * self.groups]
                )

    def sweep(self, low, high, read, write, scale=None):
        before = None
        here = read(low - 1)
        for row in range(low - 1, high):
            below = read(row + 1)
            down = [b - h for b, h in zip(below, here)]
            if scale is not None:
                down = [d * scale(row) for d in down]
            near = pltpu.roll(here[0], self.lanes - 1, 1)
            near = jnp.where(self.at_right, pltpu.roll(near, self.lines - 1, 0), near)
            across = [n - h for n, h in zip(here[1:] + [near], here)]
            across[-1] = across[-1] * self.inner
            power = [d * d + a * a for d, a in zip(down, across)]
            inverse = [lax.rsqrt(p + pltpu.roll(p, self.groups, 0) + 1.0) for p in power]
            flux = [d * i for d, i in zip(down, inverse)]
            if before is not None:
                sides = [a * i for a, i in zip(across, inverse)]
                near = pltpu.roll(sides[-1], 1, 1)
                near = jnp.where(self.at_left, pltpu.roll(near, 1, 0), near)
                fresh = [
                    h + 0.2 * (f - b + s1 - s0)
                    for h, f, b, s1, s0 in zip(here, flux, before, sides, [near] + sides[:-1])
                ]
                write(row, here, fresh)
            before = flux
            here = below


def read_row(ref, *at):
    return [ref[(*at, m)] for m in range(WAYS)]


def write_row(ref, values, *at):
    for m in range(WAYS):
        ref[(*at, m)] = values[m]


def near_kernel(shape, skipped, own_ref, core_ref, out_ref, edge_ref, field):
    tiles = Tiles(shape)
    rows, depth, halo = tiles.rows, tiles.depth, ITERS
    out_ref[...] = jnp.zeros_like(out_ref)

    def on(upper):
        def one_slice(s, carry):
            for step in range(1, ITERS + 1):
                low, high = (step, rows + ITERS - step) if upper else (step - ITERS, rows - step)
                side, kept = (low - 1, low) if upper else (high, high - 1)

                def read(row):
                    if step > 1:
                        return [field[row + halo, m] for m in range(WAYS)]
                    if 0 <= row < rows:
                        return tiles.load(own_ref, row * depth + s)
                    return tiles.load(core_ref, ((row - rows) if upper else (row + rows)) * depth - (0 if upper else skipped) + s)

                def seen(row):
                    values = read(row)
                    if row == side:
                        for m in range(WAYS):
                            edge_ref[s, step - 1, 0, m] = values[m]
                    return values

                def write(row, here, fresh):
                    if row == kept:
                        for m in range(WAYS):
                            edge_ref[s, step - 1, 1, m] = here[m]
                    if step == ITERS:
                        tiles.store(out_ref, s, row, fresh)
                    else:
                        for m in range(WAYS):
                            field[row + halo, m] = fresh[m]

                tiles.sweep(low, high, seen, write)
            return carry

        lax.fori_loop(0, depth, one_slice, 0)

    core = lax.rem(lax.axis_index("scan"), 2)
    pl.when(core == 0)(lambda: on(True))
    pl.when(core == 1)(lambda: on(False))


def far_kernel(shape, skipped, chip_ref, edge_ref, done_ref, out_ref, field):
    tiles = Tiles(shape)
    rows, depth, halo = tiles.rows, tiles.depth, ITERS
    many = field.shape[0]
    me = lax.axis_index("scan")
    upper = lax.rem(me, 2) == 0
    stop = jnp.where(me == 0, halo - 1, jnp.where(me == lax.axis_size("scan") - 1, halo + rows - 1, -1))
    out_ref[...] = done_ref[...]

    def some_slices(group, carry):
        for i in range(many):
            for row in range(halo):
                at = jnp.where(upper, (row + rows - halo) * depth - skipped, row * depth)
                write_row(
                    field, tiles.load(chip_ref, at + group * many + i), i, jnp.where(upper, 0, rows + halo) + row
                )

        def one_step(step, carry):
            low = jnp.where(upper, step - ITERS, rows - step) + halo
            side = jnp.where(upper, low + ITERS - 1, low)
            kept = jnp.where(upper, low + ITERS, low - 1)
            for i in range(many):
                s = group * many + i
                write_row(field, read_row(edge_ref, s, step - 1, 0), i, side)
                write_row(field, read_row(edge_ref, s, step - 1, 1), i, kept)
            for i in range(many):
                tiles.sweep(
                    0,
                    ITERS,
                    lambda row, i=i: read_row(field, i, low + row),
                    lambda row, here, fresh, i=i: write_row(field, fresh, i, low + row),
                    lambda row: jnp.where(low + row == stop, 0.0, 1.0),
                )
            return carry

        lax.fori_loop(1, ITERS + 1, one_step, 0)

        def one_row(row, carry):
            at = jnp.where(upper, 0, rows - ITERS) + row
            for i in range(many):
                tiles.store(out_ref, group * many + i, at, read_row(field, i, at + halo))
            return carry

        lax.fori_loop(0, ITERS, one_row, 0)
        return carry

    lax.fori_loop(0, depth // many, some_slices, 0)


def copy_kernel(plan, source_ref, *refs):
    count = len(plan)
    sems = refs[count]
    me = lax.axis_index("scan")
    core, y, x = lax.rem(me, 2), lax.rem(me // 2, 2), me // 4
    chips = source_ref.shape[2]
    copies = []
    for out, (theirs, pieces) in zip(refs, plan):
        whose = 1 - core if theirs else core
        for slot, (part, k, e) in enumerate(pieces):
            copies.append(
                pltpu.make_async_copy(
                    source_ref.at[part, :, lax.rem(x + k, chips), 1 - y if e else y, whose],
                    out.at[slot],
                    sems.at[len(copies)],
                )
            )
    for copy in copies:
        copy.start()
    for copy in copies:
        copy.wait()


def copied(split, *plan):
    _, depth, _, _, _, rows, width = split.shape
    moved = 4 * sum(len(pieces) for _, pieces in plan) * depth * rows * width
    return pl.pallas_call(
        lambda *refs: copy_kernel(plan, *refs),
        out_shape=[jax.ShapeDtypeStruct((len(pieces), depth, rows, width), split.dtype) for _, pieces in plan],
        in_specs=[pl.BlockSpec(memory_space=pltpu.HBM)],
        out_specs=[pl.BlockSpec(memory_space=pltpu.VMEM)] * len(plan),
        scratch_shapes=[pltpu.SemaphoreType.DMA((sum(len(pieces) for _, pieces in plan),))],
        cost_estimate=pl.CostEstimate(flops=0, bytes_accessed=moved, transcendentals=0),
        compiler_params=pltpu.CompilerParams(vmem_limit_bytes=moved + 2 * 1024 * 1024),
    )(split)


def on_device(partials, inverses, classes):
    _, parts, depth, rows_total, width = partials.shape
    scans = lax.axis_size("scan")
    cuts = lax.axis_size("cuts")
    rows = rows_total // scans
    lanes = width // cuts
    kinds, total, _ = inverses.shape
    chips = scans // 4
    f32, f16 = jnp.float32, jnp.float16

    def send(array, target, turn=0):
        pairs = [(i, target(i)) for i in range(scans)]
        return lax.ppermute(array, "scan", pairs[turn:] + pairs[:turn])

    def other_core(i):
        return i ^ 1

    def other_y(i):
        return i ^ 2

    def along_x(k):
        return lambda i: (i + 4 * k) % scans

    def paired(own, got):
        return (own.astype(f32) + got.astype(f32)) * SUM_SCALE

    def after(value, made):
        return lax.optimization_barrier((value, made))[0]

    split = partials.reshape(parts, depth, chips, 2, 2, rows, width)
    split = pltpu.with_memory_space_constraint(split, pltpu.HBM)
    early = [(0, 2, 0), (0, 2, 1), (1, 2, 1), (1, 0, 1)]
    late = [(1, 1, 1), (1, 3, 1)] + [(0, k, e) for k in (1, 3, 0) for e in range(2)] + [(1, k, 0) for k in (2, 0, 1, 3)]
    give_early, own_early = copied(split, (True, early), (False, early))
    got_early = send(give_early, other_core)
    give_late, own_late = copied(split, (True, late), (False, late))
    got_late = send(after(give_late, got_early), other_core, 1)

    two_steps = paired(own_early[:2], got_early[:2]).astype(f16)
    y_far = paired(own_early[2:], got_early[2:]).astype(f16)
    came_far = send(y_far, other_y)
    from_left = send(two_steps[0], along_x(1))
    from_right = send(two_steps[1], along_x(3))

    y_near = paired(own_late[:2], got_late[:2]).astype(f16)
    came_near = send(y_near, other_y, 1)
    one_step = paired(own_late[2:6], got_late[2:6])
    mine0 = paired(own_late[6:8], got_late[6:8])
    mine1 = paired(own_late[8:], got_late[8:])

    from_left, from_right = after((from_left, from_right), y_near)
    to_right = jnp.stack([one_step[0] + from_left.astype(f32), one_step[1]]).astype(f16)
    to_left = jnp.stack([one_step[2], one_step[3] + from_right.astype(f32)]).astype(f16)
    x_left = send(to_right, along_x(1))
    x_right = send(to_left, along_x(3))

    came_far = after(came_far, (to_right, to_left))
    far1 = mine1[:2] + came_far.astype(f32)
    two_steps1 = far1[0].astype(f16)
    half = depth // 2
    from_left1 = send(two_steps1[:half], along_x(1), 1)
    from_right1 = send(two_steps1[half:], along_x(3), 1)

    x_left, x_right = after((x_left, x_right), two_steps1)
    over_x = mine0 + x_left.astype(f32) + x_right.astype(f32)
    last = over_x[1].astype(f16)
    part0 = over_x[0] + send(last, other_y, 2).astype(f32)

    came_near, from_left1, from_right1 = after((came_near, from_left1, from_right1), last)
    near1 = mine1[2:] + came_near.astype(f32)
    to_right1 = jnp.concatenate([near1[0, :half] + from_left1.astype(f32), near1[0, half:]]).astype(f16)
    to_left1 = jnp.concatenate([near1[1, :half], near1[1, half:] + from_right1.astype(f32)]).astype(f16)
    x_left1 = send(to_right1, along_x(1), 2)
    x_right1 = send(to_left1, along_x(3), 2)
    part1 = far1[1] + x_left1.astype(f32) + x_right1.astype(f32)

    grad = (jnp.stack([part0, part1]) * (1.0 / SUM_SCALE)).astype(jnp.bfloat16)
    grad = grad.reshape(parts, depth, rows, cuts, lanes).transpose(3, 0, 1, 2, 4)
    weights = after(inverses, last).reshape(kinds, cuts, depth, total).transpose(2, 1, 0, 3).reshape(total, kinds * total)
    upper = lax.axis_index("scan") & 1 == 0
    grad, weights, upper = lax.optimization_barrier((grad, weights, upper))
    grad = lax.all_to_all(grad, "cuts", 0, 0, tiled=True)
    per = rows * parts * depth
    filtered = pl.pallas_call(
        filter_kernel,
        out_shape=jax.ShapeDtypeStruct((cuts * per, lanes), f32),
        scratch_shapes=[pltpu.VMEM((parts, total * rows, lanes), f32)],
        compiler_params=pltpu.CompilerParams(vmem_limit_bytes=16 * 1024 * 1024),
    )(grad, weights, classes)
    coded = (filtered * SCALE).astype(f16).reshape(cuts, per, lanes)
    coded = lax.all_to_all(coded, "cuts", 0, 0, tiled=True)
    coded = coded.reshape(cuts, parts, rows * depth, lanes)
    skipped = (rows - ITERS) * depth // TILE * TILE
    needed = -(-ITERS * depth // TILE) * TILE
    top, bottom = coded[:, :, :needed], coded[:, :, skipped:]
    odds = range(1, scans - 1, 2)
    chip = lax.ppermute(
        jnp.where(upper, top, bottom), "scan", [(i, i + 1) for i in odds] + [(i + 1, i) for i in odds]
    )

    def plain(array):
        return (array.astype(f32) * (1.0 / SCALE)).transpose(1, 0, 2, 3).reshape(-1, lanes)

    middle = plain(coded)
    core = send(after(jnp.where(upper, bottom, top), middle), other_core)
    shape = (cuts, parts, depth, rows, lanes)
    lines = parts * cuts // WAYS
    out = jax.ShapeDtypeStruct((parts * depth, cuts * rows, lanes), f32)
    field = pltpu.VMEM((rows + 2 * ITERS, WAYS, lines, lanes), f32)
    work = cuts * rows * parts * depth * lanes
    done, edges = pl.pallas_call(
        lambda *refs: near_kernel(shape, skipped, *refs),
        out_shape=[out, jax.ShapeDtypeStruct((depth, ITERS, 2, WAYS, lines, lanes), f32)],
        scratch_shapes=[field],
        cost_estimate=pl.CostEstimate(flops=0, bytes_accessed=16 * work, transcendentals=0),
        compiler_params=pltpu.CompilerParams(vmem_limit_bytes=12 * 1024 * 1024),
    )(middle, plain(core))
    chip, edges, done = lax.optimization_barrier((chip, edges, done))
    result = pl.pallas_call(
        lambda *refs: far_kernel(shape, skipped, *refs),
        out_shape=out,
        scratch_shapes=[pltpu.VMEM((MANY, rows + 2 * ITERS, WAYS, lines, lanes), f32)],
        compiler_params=pltpu.CompilerParams(vmem_limit_bytes=12 * 1024 * 1024),
    )(plain(chip), edges, done)
    result = result.reshape(parts, depth, cuts, rows, lanes).transpose(0, 1, 3, 2, 4)
    return result.reshape(parts, depth, rows, width)


def solution(mesh):
    placed = (P("scan", None, "cuts", None, None), P(), P("scan", "cuts"))
    return jax.shard_map(
        on_device,
        mesh=mesh,
        in_specs=placed,
        out_specs=P(None, "cuts", "scan", None),
        check_vma=False,
    )
```
